256 devices in a mesh: block: 16 (over y, x), space: 16 (over z, core).
Axes of the slice: x: 4, y: 4, z: 8, core: 2. Of those that a mesh axis runs over, the one named last changes fastest.
Arguments:
- video: bfloat16 [32, 4, 32, 128, 128], P('block', None, 'space'), may hold values from -6 to 6
- pred_slot: int32 [32], P('block'), may hold values from -1 to 30, as said below
- frames: int32 [32], P('block'), may hold values from 0 to 4, as said below
- gain_one: float32 [128], replicated, may hold values from 0.1 to 1.9
- conv_one: bfloat16 [3, 3, 3, 128, 128], replicated, may hold values from -0.109375 to 0.109375
- bias_one: float32 [128], replicated, may hold values from -3 to 3
- gain_two: float32 [128], replicated, may hold values from 0.1 to 1.9
- conv_two: bfloat16 [3, 3, 3, 128, 128], replicated, may hold values from -0.109375 to 0.109375
- bias_two: float32 [128], replicated, may hold values from -3 to 3
- down_weight: bfloat16 [3, 3, 3, 128, 256], replicated, may hold values from -0.109375 to 0.109375
- down_bias: float32 [256], replicated, may hold values from -3 to 3
Outputs:
- latent: bfloat16 [32, 2, 16, 64, 256], P('block', None, 'space')
The draws below stay inside these ranges and needn't reach their ends.
Inputs may be any that keep to these rules, and one draw needn't show every extreme that they name: pred_slot[s] is -1 for the first block of a video and for empty slots; otherwise it is the previous live slot in slot order: slot s - 1 on the same index of block, or the last live slot of the previous index of block for the first slot of an index. A block that is some slot's predecessor has 4 live frames. Live slots come first on every index of block, and every index holds at least one; an empty slot has 0 frames, a block with a successor 4, a video's last block 1 to 4. Frames past the live ones hold padding.
All inputs are finite; a program needn't handle non-finite values.
Results may differ from the reference program's by a relative error of at most 0.0051.
Values may be sent and summed in bfloat16 or wider, within the bound.
No kernel may reach another device: no remote copies, remote signals or barrier semaphores. Data moves between devices by JAX's collectives and lax.ppermute only.
A program may use at most 64 MiB of HBM per device.

```python
import jax
import jax.numpy as jnp
from jax import lax

C = 128
C2 = 256
F = 4
W = 128
CH_DEV = 2
SLOTS = 32
H = 32
N_BLOCK = 16


def layout(key):
    count_key, start_key, frame_key = jax.random.split(key, 3)
    counts = jax.random.randint(count_key, (N_BLOCK,), 1, CH_DEV + 1)
    counts = counts.at[0].set(CH_DEV)
    counts = counts.at[1].set(1)
    counts = counts.at[N_BLOCK - 1].set(CH_DEV)
    slot_index = jnp.arange(SLOTS, dtype=jnp.int32)
    owners = slot_index // CH_DEV
    position = slot_index % CH_DEV
    is_live = position < counts[owners]
    starts = jax.random.randint(start_key, (SLOTS,), 0, 10) < 3
    starts = starts.at[1].set(False)
    starts = starts.at[SLOTS - 1].set(False)
    earlier = jnp.where(owners > 0, (owners - 1) * CH_DEV + counts[jnp.maximum(owners - 1, 0)] - 1, -1)
    previous = jnp.where(position > 0, slot_index - 1, earlier)
    pred_slot = jnp.where(is_live & jnp.logical_not(starts), previous, -1).astype(jnp.int32)
    targets = jnp.where(pred_slot >= 0, pred_slot, SLOTS)
    continued = jnp.zeros((SLOTS,), jnp.int32).at[targets].set(1, mode='drop')
    short_len = jax.random.randint(frame_key, (SLOTS,), 1, F + 1)
    frames = jnp.where(is_live, jnp.where(continued > 0, F, short_len), 0).astype(jnp.int32)
    return (pred_slot, frames)


def draw_pred_slot(key, part):
    return layout(key)[0]


def draw_frames(key, part):
    return layout(key)[1]


def block_levels(key, extent, shards, smallest, high):
    loudness = 1.0
    for dim, parts in shards:
        steps = jax.random.uniform(jax.random.fold_in(jax.random.fold_in(key, 6), dim), (parts,), jnp.float32, smallest / len(shards), high / len(shards))
        loudness = loudness * jnp.repeat(jnp.exp(steps), extent[dim] // parts).reshape((-1,) + (1,) * (len(extent) - 1 - dim))
    return loudness


def scatter_about(key, dims, width, most, pieces=(), held_as=jnp.bfloat16):
    loudness = block_levels(key, dims, pieces, -0.22, 0.18) if pieces else 1.0
    entries = jax.random.normal(key, dims, jnp.float32) * width * loudness
    return jnp.minimum(jnp.maximum(entries, -most), most).astype(held_as)


def setup_inputs(seed: int = 0) -> dict:
    key_of = jax.random.split(jax.random.key(seed), 12)
    video = scatter_about(key_of[0], (SLOTS, F, H, W, C), 1.0, 6.0, ((0, 16), (2, 16)))
    pred_slot = draw_pred_slot(jax.random.fold_in(key_of[11], 71), 0)
    frames = draw_frames(jax.random.fold_in(key_of[11], 71), 0)
    gain_one = jnp.clip(1.0 + 0.18 * jax.random.normal(key_of[3], (C,), jnp.float32), 0.1, 1.9)
    conv_one = scatter_about(key_of[4], (3, 3, 3, C, C), (27 * C) ** -0.5, 0.109375)
    bias_one = scatter_about(key_of[5], (C,), 0.5, 3.0, (), jnp.float32)
    gain_two = jnp.clip(1.0 + 0.18 * jax.random.normal(key_of[6], (C,), jnp.float32), 0.1, 1.9)
    conv_two = scatter_about(key_of[7], (3, 3, 3, C, C), (27 * C) ** -0.5, 0.109375)
    bias_two = scatter_about(key_of[8], (C,), 0.5, 3.0, (), jnp.float32)
    down_weight = scatter_about(key_of[9], (3, 3, 3, C, C2), (27 * C) ** -0.5, 0.109375)
    down_bias = scatter_about(key_of[10], (C2,), 0.5, 3.0, (), jnp.float32)
    return dict(video=video, pred_slot=pred_slot, frames=frames, gain_one=gain_one, conv_one=conv_one, bias_one=bias_one, gain_two=gain_two, conv_two=conv_two, bias_two=bias_two, down_weight=down_weight, down_bias=down_bias)


def activate(values, gain):
    values = values.astype(jnp.float32)
    scaled = values * lax.rsqrt(lax.optimization_barrier(jnp.mean(values * values, axis=-1, keepdims=True)) + 1e-06) * gain
    return jax.nn.silu(scaled)

def contexts(activity, pred_slot):
    tail_frames = activity[:, F - 2:]
    picked = tail_frames[jnp.maximum(pred_slot, 0).astype(jnp.int32)]
    keep = (pred_slot >= 0)[:, None, None, None, None]
    return jnp.where(keep, picked, jnp.zeros_like(picked))

def convolve(extended, weight, strides):
    result = lax.conv_general_dilated(extended.astype(jnp.float32)[None], weight.astype(jnp.float32), strides, ((0, 0), (1, 1), (1, 1)), dimension_numbers=('NDHWC', 'DHWIO', 'NDHWC'), precision=lax.Precision.HIGHEST)
    return result[0]

def layer(activity, pred_slot, weight, strides):
    context = contexts(activity, pred_slot)

    def single(pair_item):
        return convolve(jnp.concatenate([pair_item[0], pair_item[1]], axis=0), weight, strides)
    return lax.map(single, (context, activity))

def reference(video, pred_slot, frames, gain_one, conv_one, bias_one, gain_two, conv_two, bias_two, down_weight, down_bias):
    first_act = activate(video, gain_one).astype(jnp.bfloat16)
    hidden_one = layer(first_act, pred_slot, conv_one, (1, 1, 1)) + bias_one
    second_act = activate(hidden_one, gain_two).astype(jnp.bfloat16)
    hidden_two = layer(second_act, pred_slot, conv_two, (1, 1, 1)) + bias_two
    summed = (video.astype(jnp.float32) + hidden_two).astype(jnp.bfloat16)
    down = layer(summed, pred_slot, down_weight, (2, 2, 2)) + down_bias
    out_frames = jnp.arange(F // 2, dtype=jnp.int32)
    keep = (2 * out_frames)[None, :] < frames[:, None]
    down = jnp.where(keep[:, :, None, None, None], down, jnp.zeros_like(down))
    return down.astype(jnp.bfloat16)
```

```python
import functools

import jax
import jax.numpy as jnp
from jax import lax
from jax.experimental import pallas as pl
from jax.experimental.pallas import tpu as pltpu
from jax.sharding import PartitionSpec as P

F32 = jnp.float32
BF16 = jnp.bfloat16
VMEM_LIMIT = 56 * 2**20


def activate(values, gain):
    values = values.astype(F32)
    mean = jnp.mean(values * values, axis=-1, keepdims=True)
    scaled = values * lax.rsqrt(mean + 1e-06) * gain
    return scaled / (1.0 + jnp.exp(-scaled))


def first_kernel(meta, video, gain, act, tail):
    for slot in range(2):
        for frame in range(4):
            act[slot, frame] = activate(video[slot, frame], gain[...]).astype(BF16)
    last = meta[2]
    tail[...] = act[last]


def pair_weight(weight, wide):
    zero = jnp.zeros((128, 128), BF16)
    for kt in range(3):
        for j in range(4):
            rows = pl.ds((kt * 4 + j) * 128, 128)
            for kw in range(3):
                for r in range(2):
                    kh = j - r
                    inside = 0 <= kh <= 2
                    wide[rows, pl.ds((kw * 2 + r) * 128, 128)] = weight[kt, kh, kw] if inside else zero


def pair_conv(source, wide, frame, count, row):
    m = count * 128
    pieces = [
        source[pl.ds(frame + kt, count), row + j].reshape(m, 128) for kt in range(3) for j in range(4)
    ]
    z = jnp.dot(jnp.concatenate(pieces, axis=1), wide[...], preferred_element_type=F32)
    left = z[:, :256].reshape(count, 128, 256)
    right = z[:, 512:].reshape(count, 128, 256)
    edge = jnp.zeros((count, 1, 256), F32)
    left = jnp.concatenate([edge, left[:, :127]], axis=1)
    right = jnp.concatenate([right[:, 1:], edge], axis=1)
    return left.reshape(m, 256) + z[:, 256:512] + right.reshape(m, 256)


def main_kernel(
    meta, own, pin, cross, pown, ppin, pcross, video, w_one, bias_one, gain_two, w_two, bias_two, w_down, bias_down,
    out, below, sent,
    ux, u2, wide, ys, total, lower,
):
    has_a, has_b, last, parity, top, bottom = (meta[i] for i in range(6))
    keep_a, keep_b = has_a > 0, has_b > 0

    def assemble(near_above, near_below, p_above, p_below):
        for k, src in ((0, p_above), (2, pown), (4, p_below)):
            for f in range(4):
                v = src[f]
                ux[f, k : k + 2] = jnp.where(keep_a, v, jnp.zeros_like(v))
        for k, src in ((0, near_above), (2, own), (4, near_below)):
            ux[4:8, k : k + 2] = src[0]
            ux[10:14, k : k + 2] = src[1]
            for f in range(2):
                v = src[0, 2 + f]
                ux[8 + f, k : k + 2] = jnp.where(keep_b, v, jnp.zeros_like(v))

    @pl.when(parity == 0)
    def _():
        assemble(cross, pin, pcross, ppin)

    @pl.when(parity != 0)
    def _():
        assemble(pin, cross, ppin, pcross)

    pair_weight(w_one, wide)
    for source, count, target in ((0, 2, 0), (2, 2, 2), (4, 2, 4), (8, 2, 8), (10, 2, 10)):
        for row in (0, 2):
            h = pair_conv(ux, wide, source, count, row)
            for r in range(2):
                v = activate(h[:, r * 128 : r * 128 + 128] + bias_one[...], gain_two[...])
                local = row + r
                if local == 0:
                    v = jnp.where(top > 0, jnp.zeros_like(v), v)
                if local == 3:
                    v = jnp.where(bottom > 0, jnp.zeros_like(v), v)
                if target == 0:
                    v = jnp.where(keep_a, v, jnp.zeros_like(v))
                v = v.astype(BF16).reshape(count, 128, 128)
                u2[target : target + 2, local] = v
                if target == 4:
                    u2[6:8, local] = jnp.where(keep_b, v, jnp.zeros_like(v))
    pair_weight(w_two, wide)
    ys[:, :, :8] = jnp.zeros((8, 2, 8, 128), F32)
    for slot in range(2):
        for half in range(2):
            h = pair_conv(u2, wide, 6 * slot + 2 * half, 2, 0)
            for r in range(2):
                v = h[:, r * 128 : r * 128 + 128] + bias_two[...]
                y = video[slot, 2 * half : 2 * half + 2, r].reshape(256, 128).astype(F32) + v
                y = y.astype(BF16).astype(F32).reshape(2, 128, 128)
                ys[4 * slot + 2 * half : 4 * slot + 2 * half + 2, r, 8:] = y

    def columns(slot, frame, r):
        at = 4 * slot + frame
        return jnp.concatenate(
            [ys[at, r, pl.ds(7 + kw, 64, stride=2)].astype(BF16) for kw in range(3)], axis=1
        )

    def gather(frames, r):
        return jnp.concatenate([columns(slot, f, r) for slot in range(2) for f in frames], axis=0)

    sums = {}
    for kt, frames, goes in ((0, (0, 2), (1, 2)), (1, (1, 3), (1, 2)), (2, (0, 2), (0, 1))):
        upper, under = gather(frames, 0), gather(frames, 1)
        here = jnp.dot(
            jnp.concatenate([upper, under], axis=1), w_down[kt, 384:], preferred_element_type=F32
        )
        next_band = jnp.dot(under, w_down[kt, :384], preferred_element_type=F32)
        for slot in range(2):
            for i, t in enumerate(goes):
                part = slice((slot * 2 + i) * 64, (slot * 2 + i) * 64 + 64)
                for name, value in (("here", here), ("next", next_band)):
                    key = (name, slot, t)
                    sums[key] = sums[key] + value[part] if key in sums else value[part]
    zero = jnp.zeros((64, 256), F32)
    sums["here", 1, 0] += jnp.where(keep_b, sums["here", 0, 2], zero)
    sums["next", 1, 0] += jnp.where(keep_b, sums["next", 0, 2], zero)
    for slot in range(2):
        for t in range(2):
            out[slot, t] = sums["here", slot, t] + bias_down[...]
            below[slot, t] = sums["next", slot, t].astype(BF16)
    sent[0] = jnp.where(last > 0, sums["here", 1, 2], sums["here", 0, 2]).astype(BF16)
    sent[1] = jnp.where(last > 0, sums["next", 1, 2], sums["next", 0, 2]).astype(BF16)


def call(kernel, outs, scratch, n_in, flops):
    vmem = pl.BlockSpec(memory_space=pltpu.VMEM)
    return pl.pallas_call(
        kernel,
        out_shape=[jax.ShapeDtypeStruct(shape, dtype) for shape, dtype in outs],
        in_specs=[pl.BlockSpec(memory_space=pltpu.SMEM)] + [vmem] * n_in,
        out_specs=[vmem] * len(outs),
        scratch_shapes=scratch,
        compiler_params=pltpu.CompilerParams(vmem_limit_bytes=VMEM_LIMIT),
        cost_estimate=pl.CostEstimate(flops=flops, bytes_accessed=2**20, transcendentals=0),
    )


def local(
    video, pred_slot, frames, gain_one, conv_one, bias_one, gain_two, conv_two, bias_two, down_weight, down_bias
):
    n_block, n_space = lax.axis_size("block"), lax.axis_size("space")
    space = lax.axis_index("space")
    has = (pred_slot >= 0).astype(jnp.int32)
    last = (frames[1] > 0).astype(jnp.int32)
    meta = jnp.stack(
        [has[0], has[1], last, space % 2, (space == 0).astype(jnp.int32), (space == n_space - 1).astype(jnp.int32)]
    )
    band = video.shape
    act, tail = call(first_kernel, [(band, BF16), (band[1:], BF16)], [], 2, 10**6)(
        meta, video, gain_one.reshape(1, 128)
    )
    inner = [(i, i ^ 1) for i in range(n_space)]
    outer = [(i, j) for i in range(n_space) if 0 <= (j := i + 1 if i % 2 else i - 1) < n_space]
    onward = [(b, b + 1) for b in range(n_block - 1)]
    corner = [(b * n_space + i, (b + 1) * n_space + j) for b in range(n_block - 1) for i, j in outer]
    pin = lax.ppermute(act, "space", inner)
    cross = lax.ppermute(act, "space", outer)
    pown = lax.ppermute(tail, "block", onward)
    pcross = lax.ppermute(tail, ("block", "space"), corner)
    ppin = lax.ppermute(pown, "space", inner)
    out, below, sent = call(
        main_kernel,
        [((2, 2, 64, 256), F32), ((2, 2, 64, 256), BF16), ((2, 64, 256), BF16)],
        [
            pltpu.VMEM((14, 6, 128, 128), BF16),
            pltpu.VMEM((12, 4, 128, 128), BF16),
            pltpu.VMEM((1536, 768), BF16),
            pltpu.VMEM((8, 2, 136, 128), F32),
            pltpu.VMEM((8, 128), F32),
            pltpu.VMEM((8, 128), F32),
        ],
        14,
        10**10,
    )(
        meta, act, pin, cross, pown, ppin, pcross, video,
        conv_one, bias_one.reshape(1, 128), gain_two.reshape(1, 128), conv_two, bias_two.reshape(1, 128),
        down_weight.reshape(3, 1152, 256), down_bias.reshape(1, 256),
    )
    got = lax.ppermute(sent, "block", onward)
    got = jnp.where(has[0] > 0, got.astype(F32), 0.0)
    first = jnp.pad(got[:, None, None], ((0, 0), (0, 1), (0, 1), (0, 0), (0, 0)))
    below = (below.astype(F32) + first[1]).astype(BF16)
    above = lax.ppermute(below, "space", [(i, i + 1) for i in range(n_space - 1)])
    down = out + above.astype(F32) + first[0]
    keep = (2 * jnp.arange(2, dtype=jnp.int32))[None, :] < frames[:, None]
    down = jnp.where(keep[:, :, None, None], down, 0.0)
    return down.astype(BF16)[:, :, None]


def solution(mesh):
    return jax.shard_map(
        local,
        mesh=mesh,
        in_specs=(P("block", None, "space", None, None), P("block"), P("block")) + (P(),) * 8,
        out_specs=P("block", None, "space", None, None),
        check_vma=False,
    )
```

```python
import jax
import jax.numpy as jnp
from jax import lax
from jax.experimental import pallas as pl
from jax.experimental.pallas import tpu as pltpu
from jax.sharding import PartitionSpec as P

F32 = jnp.float32
BF16 = jnp.bfloat16
VMEM_LIMIT = 26 * 2**20
OWN = 10**9
SECOND = 10**9


def activate(values, gain):
    values = values.astype(F32)
    mean = jnp.mean(values * values, axis=-1, keepdims=True)
    scaled = values * lax.rsqrt(mean + 1e-06) * gain
    return scaled / (1.0 + jnp.exp(-scaled))


def masked(keep, value):
    return jnp.where(keep, value, jnp.zeros_like(value))


def first_kernel(frames, video, gain, act, tail):
    for slot in range(2):
        for frame in range(4):
            act[slot, frame] = activate(video[slot, frame], gain[...]).astype(BF16)
    tail[...] = act[jnp.where(frames[1] > 0, 1, 0)]


def pair_weight(weight, wide):
    zero = jnp.zeros((128, 128), BF16)
    for kt in range(3):
        for j in range(4):
            rows = pl.ds((kt * 4 + j) * 128, 128)
            for kw in range(3):
                for r in range(2):
                    kh = j - r
                    inside = 0 <= kh <= 2
                    wide[rows, pl.ds((kw * 2 + r) * 128, 128)] = weight[kt, kh, kw] if inside else zero


def weight_kernel(w_one, w_two, wide, wide_two):
    pair_weight(w_one, wide)
    pair_weight(w_two, wide_two)


def pair_conv(source, wide, frame, count, row):
    m = count * 128
    pieces = [
        source[pl.ds(frame + kt, count), row + j].reshape(m, 128) for kt in range(3) for j in range(4)
    ]
    z = jnp.dot(jnp.concatenate(pieces, axis=1), wide[...], preferred_element_type=F32)
    left = z[:, :256].reshape(count, 128, 256)
    right = z[:, 512:].reshape(count, 128, 256)
    edge = jnp.zeros((count, 1, 256), F32)
    left = jnp.concatenate([edge, left[:, :127]], axis=1)
    right = jnp.concatenate([right[:, 1:], edge], axis=1)
    return left.reshape(m, 256) + z[:, 256:512] + right.reshape(m, 256)


def hidden_rows(ux, wide, bias, gain, frame, row):
    space = lax.axis_index("space")
    h = pair_conv(ux, wide, frame, 2, row)
    for r in range(2):
        v = activate(h[:, r * 128 : r * 128 + 128] + bias[...], gain[...])
        if row + r == 0:
            v = masked(space > 0, v)
        if row + r == 3:
            v = masked(space < lax.axis_size("space") - 1, v)
        yield row + r, v.astype(BF16).reshape(2, 128, 128)


def summed_rows(u2, wide, bias, frame, video, slot, first, ys, at):
    h = pair_conv(u2, wide, frame, 2, 0)
    for r in range(2):
        v = h[:, r * 128 : r * 128 + 128] + bias[...]
        y = video[slot, first : first + 2, r].reshape(256, 128).astype(F32) + v
        ys[at : at + 2, r, 8:] = y.astype(BF16).astype(F32).reshape(2, 128, 128)


def strided(ys, w_down):
    def gather(frames, r):
        return jnp.concatenate(
            [
                jnp.concatenate([ys[f, r, pl.ds(7 + kw, 64, stride=2)].astype(BF16) for kw in range(3)], axis=1)
                for f in frames
            ],
            axis=0,
        )

    here, below = {}, {}
    for kt, frames, goes in ((0, (0, 2), (1, 2)), (1, (1, 3), (1, 2)), (2, (0, 2), (0, 1))):
        upper, under = gather(frames, 0), gather(frames, 1)
        parts = (
            (here, jnp.dot(jnp.concatenate([upper, under], axis=1), w_down[kt, 384:], preferred_element_type=F32)),
            (below, jnp.dot(under, w_down[kt, :384], preferred_element_type=F32)),
        )
        for i, t in enumerate(goes):
            for sums, value in parts:
                part = value[i * 64 : i * 64 + 64]
                sums[t] = sums[t] + part if t in sums else part
    return here, below


def fill(ux, first, count, own, above, below, take):
    for k, src in ((0, above), (2, own), (4, below)):
        for f in range(count):
            ux[first + f, k : k + 2] = take(src, f)


def by_parity(body, pin, cross):
    parity = lax.rem(lax.axis_index("space"), 2)

    @pl.when(parity == 0)
    def _():
        body(cross, pin)

    @pl.when(parity != 0)
    def _():
        body(pin, cross)


def own_kernel(pred, own, pin, cross, wide, bias_one, gain_two, u2a, u2b, ux):
    keep = pred[1] >= 0

    def assemble(above, below):
        fill(ux, 0, 4, own, above, below, lambda src, f: src[0, f])
        fill(ux, 4, 2, own, above, below, lambda src, f: masked(keep, src[0, 2 + f]))
        fill(ux, 6, 4, own, above, below, lambda src, f: src[1, f])

    by_parity(assemble, pin, cross)
    for frame, target in ((0, 0), (4, 2), (6, 4)):
        for row in (0, 2):
            for at, v in hidden_rows(ux, wide, bias_one, gain_two, frame, row):
                if target == 0:
                    u2a[:, at] = v
                    v = masked(keep, v)
                u2b[target : target + 2, at] = v


def second_kernel(u2, video, wide_two, bias_two, w_down, bias_down, here_b, below_b, sent_b, ys):
    ys[:, :, :8] = jnp.zeros((4, 2, 8, 128), F32)
    for half in range(2):
        summed_rows(u2, wide_two, bias_two, 2 * half, video, 1, 2 * half, ys, 2 * half)
    here, below = strided(ys, w_down)
    for t in range(2):
        here_b[t] = here[t] + bias_down[...]
        below_b[t] = below[t]
    sent_b[0] = here[2]
    sent_b[1] = below[2]


def rest_kernel(
    pred, frames, own, pin, cross, pown, ppin, pcross, u2a, here_b, below_b, sent_b, video,
    wide, bias_one, gain_two, wide_two, bias_two, w_down, bias_down,
    out, below_out, sent,
    ux, u2, ys,
):
    keep_a, keep_b = pred[0] >= 0, pred[1] >= 0

    def assemble_own(above, below):
        fill(ux, 4, 2, own, above, below, lambda src, f: src[0, f])

    def assemble_before(above, below):
        fill(ux, 0, 4, pown, above, below, lambda src, f: masked(keep_a, src[f]))

    by_parity(assemble_own, pin, cross)
    by_parity(assemble_before, ppin, pcross)
    ys[:, :, :8] = jnp.zeros((4, 2, 8, 128), F32)
    u2[4:6] = u2a[...]
    for frame, target in ((0, 0), (2, 2)):
        for row in (0, 2):
            for at, v in hidden_rows(ux, wide, bias_one, gain_two, frame, row):
                u2[target : target + 2, at] = masked(keep_a, v) if target == 0 else v
    for half in (1, 0):
        summed_rows(u2, wide_two, bias_two, 2 * half, video, 0, 2 * half, ys, 2 * half)
    here, below = strided(ys, w_down)
    for t in range(2):
        out[0, t] = here[t] + bias_down[...]
        below_out[0, t] = below[t]
    out[1, 0] = here_b[0] + masked(keep_b, here[2])
    out[1, 1] = here_b[1]
    below_out[1, 0] = below_b[0] + masked(keep_b, below[2])
    below_out[1, 1] = below_b[1]
    second = frames[1] > 0
    sent[0] = jnp.where(second, sent_b[0], here[2]).astype(BF16)
    sent[1] = jnp.where(second, sent_b[1], below[2]).astype(BF16)


def relay_kernel(pred, got, below, below_out):
    below_out[...] = below[...].astype(BF16)
    below_out[0, 0] = (below[0, 0] + masked(pred[0] >= 0, got[1].astype(F32))).astype(BF16)


def last_kernel(pred, frames, here, got, above, out):
    for slot in range(2):
        for t in range(2):
            v = here[slot, t] + above[slot, t].astype(F32)
            if slot == 0 and t == 0:
                v = v + masked(pred[0] >= 0, got[0].astype(F32))
            out[slot, t, 0] = masked(2 * t < frames[slot], v).astype(BF16)


VMEM = pl.BlockSpec(memory_space=pltpu.VMEM)
SMEM = pl.BlockSpec(memory_space=pltpu.SMEM)


def call(kernel, outs, scratch, scalars, arrays, flops, limit=VMEM_LIMIT):
    return pl.pallas_call(
        kernel,
        out_shape=[jax.ShapeDtypeStruct(shape, dtype) for shape, dtype in outs],
        in_specs=[SMEM] * len(scalars) + [VMEM] * len(arrays),
        out_specs=[VMEM] * len(outs),
        scratch_shapes=scratch,
        compiler_params=pltpu.CompilerParams(vmem_limit_bytes=limit),
        cost_estimate=pl.CostEstimate(flops=flops, bytes_accessed=2**18, transcendentals=0),
    )(*scalars, *arrays)


def local(
    video, pred_slot, frames, gain_one, conv_one, bias_one, gain_two, conv_two, bias_two, down_weight, down_bias
):
    n_block, n_space = lax.axis_size("block"), lax.axis_size("space")
    band = video.shape
    act, tail = call(
        first_kernel, [(band, BF16), (band[1:], BF16)], [], (frames,), (video, gain_one.reshape(1, 128)), 10**9,
        60 * 2**20,
    )
    inner = [(i, i ^ 1) for i in range(n_space)]
    outer = [(i, j) for i in range(n_space) if 0 <= (j := i + 1 if i % 2 else i - 1) < n_space]
    onward = [(b, b + 1) for b in range(n_block - 1)]
    corner = [(b * n_space + i, (b + 1) * n_space + j) for b in range(n_block - 1) for i, j in outer]
    pown = lax.ppermute(tail, "block", onward)
    pin = lax.ppermute(act, "space", inner)
    cross = lax.ppermute(act, "space", outer)
    pcross = lax.ppermute(tail, ("block", "space"), corner)
    wide = ((1536, 768), BF16)
    conv_one, pown = lax.optimization_barrier((conv_one, pown))
    wide_one, wide_two = call(weight_kernel, [wide, wide], [], (), (conv_one, conv_two), 10**10)
    norm = (wide_one, bias_one.reshape(1, 128), gain_two.reshape(1, 128))
    stride = (wide_two, bias_two.reshape(1, 128), down_weight.reshape(3, 1152, 256), down_bias.reshape(1, 256))
    ys = pltpu.VMEM((4, 2, 136, 128), F32)
    one = ((2, 64, 256), F32)
    both = ((2, 2, 64, 256), F32)
    u2a, u2b = call(
        own_kernel, [((2, 4, 128, 128), BF16), ((6, 4, 128, 128), BF16)], [pltpu.VMEM((10, 6, 128, 128), BF16)],
        (pred_slot,), (act, pin, cross, *norm), OWN,
    )
    ppin = lax.ppermute(pown, "space", inner)
    here_b, below_b, sent_b = call(second_kernel, [one, one, one], [ys], (), (u2b, video, *stride), SECOND)
    out, below, sent = call(
        rest_kernel, [both, both, ((2, 64, 256), BF16)],
        [pltpu.VMEM((6, 6, 128, 128), BF16), pltpu.VMEM((6, 4, 128, 128), BF16), ys], (pred_slot, frames),
        (act, pin, cross, pown, ppin, pcross, u2a, here_b, below_b, sent_b, video, *norm, *stride), 5 * 10**9,
    )
    got = lax.ppermute(sent, "block", onward)
    [below] = call(relay_kernel, [(both[0], BF16)], [], (pred_slot,), (got, below), 10**6)
    above = lax.ppermute(below, "space", [(i, i + 1) for i in range(n_space - 1)])
    [down] = call(last_kernel, [((2, 2, 1, 64, 256), BF16)], [], (pred_slot, frames), (out, got, above), 10**6)
    return down


def solution(mesh):
    return jax.shard_map(
        local,
        mesh=mesh,
        in_specs=(P("block", None, "space", None, None), P("block"), P("block")) + (P(),) * 8,
        out_specs=P("block", None, "space", None, None),
        check_vma=False,
    )
```

```python
import jax
import jax.numpy as jnp
from jax import lax
from jax.experimental import pallas as pl
from jax.experimental.pallas import tpu as pltpu
from jax.sharding import PartitionSpec as P

F32 = jnp.float32
BF16 = jnp.bfloat16
VMEM_LIMIT = 26 * 2**20
WEIGHT = 3 * 10**9
MID = 2 * 10**9
OUTER = 2 * 10**10
SECOND = 2 * 10**9


def activate(values, gain):
    values = values.astype(F32)
    mean = jnp.mean(values * values, axis=-1, keepdims=True)
    scaled = values * lax.rsqrt(mean + 1e-06) * gain
    return scaled / (1.0 + jnp.exp(-scaled))


def masked(keep, value):
    return jnp.where(keep, value, jnp.zeros_like(value))


def pair_weight(weight, wide):
    zero = jnp.zeros((128, 128), BF16)
    for kt in range(3):
        for j in range(4):
            rows = pl.ds((kt * 4 + j) * 128, 128)
            for kw in range(3):
                for r in range(2):
                    kh = j - r
                    inside = 0 <= kh <= 2
                    wide[rows, pl.ds((kw * 2 + r) * 128, 128)] = weight[kt, kh, kw] if inside else zero


def weight_kernel(w_one, w_two, wide, wide_two):
    pair_weight(w_one, wide)
    pair_weight(w_two, wide_two)


def pair_conv(source, wide, frame, count, row):
    m = count * 128
    pieces = [
        source[pl.ds(frame + kt, count), row + j].reshape(m, 128) for kt in range(3) for j in range(4)
    ]
    z = jnp.dot(jnp.concatenate(pieces, axis=1), wide[...], preferred_element_type=F32)
    left = z[:, :256].reshape(count, 128, 256)
    right = z[:, 512:].reshape(count, 128, 256)
    edge = jnp.zeros((count, 1, 256), F32)
    left = jnp.concatenate([edge, left[:, :127]], axis=1)
    right = jnp.concatenate([right[:, 1:], edge], axis=1)
    return left.reshape(m, 256) + z[:, 256:512] + right.reshape(m, 256)


def first_kernel(frames, video, gain, act, tail):
    for slot in range(2):
        for frame in range(4):
            act[slot, frame] = activate(video[slot, frame], gain[...]).astype(BF16)
    tail[...] = act[jnp.where(frames[1] > 0, 1, 0)]


def hidden_rows(source, wide, bias, gain, frame, row):
    h = pair_conv(source, wide, frame, 2, row)
    for r in range(2):
        v = activate(h[:, r * 128 : r * 128 + 128] + bias[...], gain[...])
        yield r, v.reshape(2, 128, 128)


def inside(value, top, bottom):
    space = lax.axis_index("space")
    if top:
        value = masked(space > 0, value)
    if bottom:
        value = masked(space < lax.axis_size("space") - 1, value)
    return value


def summed_rows(u2, wide, bias, frame, video, slot, first, ys, at):
    h = pair_conv(u2, wide, frame, 2, 0)
    for r in range(2):
        v = h[:, r * 128 : r * 128 + 128] + bias[...]
        y = video[slot, first : first + 2, r].reshape(256, 128).astype(F32) + v
        ys[pl.ds(at, 2), r, 8:] = y.astype(BF16).astype(F32).reshape(2, 128, 128)


def columns(ys, frame, r):
    return jnp.concatenate([ys[frame, r, pl.ds(7 + kw, 64, stride=2)].astype(BF16) for kw in range(3)], axis=1)


def mid_kernel(pred, own, pin, wide, bias_one, gain_two, near, mid):
    keep = pred[1] >= 0
    parity = lax.rem(lax.axis_index("space"), 2)
    for src, at in ((own, 2 * parity), (pin, 2 - 2 * parity)):
        for slot in range(2):
            for f in range(4):
                v = src[slot, f]
                near[6 * slot + f, pl.ds(at, 2)] = v
                if slot == 0 and f >= 2:
                    near[2 + f, pl.ds(at, 2)] = masked(keep, v)
    for frame, target in ((0, 0), (4, 2), (6, 4)):
        for r, v in hidden_rows(near, wide, bias_one, gain_two, frame, 0):
            mid[target : target + 2, r] = v.astype(BF16)


def outer_kernel(pred, near, mid, cross, wide, bias_one, gain_two, u2a, u2b, ux):
    keep = pred[1] >= 0
    parity = lax.rem(lax.axis_index("space"), 2)
    at, other = 2 * parity, 2 - 2 * parity
    ux[:, pl.ds(other, 2)] = near[:, pl.ds(at, 2)]
    for slot in range(2):
        for f in range(4):
            v = cross[slot, f]
            ux[6 * slot + f, pl.ds(at, 2)] = v
            if slot == 0 and f >= 2:
                ux[2 + f, pl.ds(at, 2)] = masked(keep, v)
    for frame, target in ((0, 0), (4, 2), (6, 4)):
        for r, v in hidden_rows(ux, wide, bias_one, gain_two, frame, 0):
            v = inside(v, r == 0, r == 1).astype(BF16)
            if target == 0:
                u2a[:, at + r] = v
                v = masked(keep, v)
            u2b[target : target + 2, at + r] = v
    u2a[:, pl.ds(other, 2)] = mid[0:2]
    u2b[0:2, pl.ds(other, 2)] = masked(keep, mid[0:2])
    u2b[2:6, pl.ds(other, 2)] = mid[2:6]


def before(refs, frame, keep, ux, at):
    parity = lax.rem(lax.axis_index("space"), 2)
    for src, row in zip(refs, (2, 4 - 4 * parity, 4 * parity)):
        ux[at, pl.ds(row, 2)] = masked(keep, src[frame])


def strided(ys, w_down):
    rows = {(f, r): columns(ys, f, r) for f in range(4) for r in range(2)}
    here, below = {}, {}
    for kt, read, goes in ((0, (0, 2), (1, 2)), (1, (1, 3), (1, 2)), (2, (0, 2), (0, 1))):
        upper, under = (jnp.concatenate([rows[f, r] for f in read], axis=0) for r in range(2))
        parts = (
            (here, jnp.dot(jnp.concatenate([upper, under], axis=1), w_down[kt, 384:], preferred_element_type=F32)),
            (below, jnp.dot(under, w_down[kt, :384], preferred_element_type=F32)),
        )
        for i, t in enumerate(goes):
            for sums, value in parts:
                part = value[i * 64 : i * 64 + 64]
                sums[t] = sums[t] + part if t in sums else part
    return here, below


def second_kernel(u2, video, wide_two, bias_two, w_down, bias_down, here_b, below_b, sent_b, ys):
    ys[:, :, :8] = jnp.zeros((4, 2, 8, 128), F32)
    for half in range(2):
        summed_rows(u2, wide_two, bias_two, 2 * half, video, 1, 2 * half, ys, 2 * half)
    here, below = strided(ys, w_down)
    for t in range(2):
        here_b[t] = here[t] + bias_down[...]
        below_b[t] = below[t]
    sent_b[0] = here[2]
    sent_b[1] = below[2]


def context_kernel(
    pred, frames, near, cross, pown, ppin, pcross, u2a, sent_b, video,
    wide, bias_one, gain_two, wide_two, bias_two, w_down,
    u2c, ya, sent,
    ux, us, ys,
):
    keep = pred[0] >= 0
    parity = lax.rem(lax.axis_index("space"), 2)
    for f in range(2):
        before((pown, ppin, pcross), 2 + f, keep, ux, f)
    ux[2:4, pl.ds(2 - 2 * parity, 4)] = near[0:2]
    ux[2:4, pl.ds(4 * parity, 2)] = cross[0, 0:2]
    us[2:4] = u2a[...]
    ys[:, :, :8] = jnp.zeros((2, 2, 8, 128), F32)
    for row in (0, 2):
        for r, v in hidden_rows(ux, wide, bias_one, gain_two, 0, row):
            us[0:2, row + r] = inside(v, row + r == 0, row + r == 3).astype(BF16)
    u2c[...] = us[0:2]
    summed_rows(us, wide_two, bias_two, 0, video, 0, 2, ys, 0)
    ya[...] = ys[...]
    here, below = 0.0, 0.0
    for kt in range(2):
        upper, under = columns(ys, kt, 0), columns(ys, kt, 1)
        both = jnp.concatenate([upper, under], axis=1)
        here = here + jnp.dot(both, w_down[kt, 384:], preferred_element_type=F32)
        below = below + jnp.dot(under, w_down[kt, :384], preferred_element_type=F32)
    second = frames[1] > 0
    sent[0] = jnp.where(second, sent_b[0], here).astype(BF16)
    sent[1] = jnp.where(second, sent_b[1], below).astype(BF16)


def rest_kernel(
    pred, pown, ppin, pcross, u2c, u2a, ya, here_b, below_b, video,
    wide, bias_one, gain_two, wide_two, bias_two, w_down, bias_down,
    out, below_out,
    ux, ua, ys,
):
    keep_a, keep_b = pred[0] >= 0, pred[1] >= 0
    for f in range(4):
        before((pown, ppin, pcross), f, keep_a, ux, f)
    ua[2:4] = u2c[...]
    ys[0:2, :, :8] = jnp.zeros((2, 2, 8, 128), F32)
    ys[2:4] = ya[...]
    for row in (0, 2):
        for r, v in hidden_rows(ux, wide, bias_one, gain_two, 0, row):
            ua[0:2, row + r] = masked(keep_a, inside(v, row + r == 0, row + r == 3)).astype(BF16)
    summed_rows(ua, wide_two, bias_two, 0, video, 0, 0, ys, 0)
    here, below = strided(ys, w_down)
    for t in range(2):
        out[0, t] = here[t] + bias_down[...]
        below_out[0, t] = below[t]
    out[1, 0] = here_b[0] + masked(keep_b, here[2])
    out[1, 1] = here_b[1]
    below_out[1, 0] = below_b[0] + masked(keep_b, below[2])
    below_out[1, 1] = below_b[1]


def relay_kernel(pred, got, below, below_out):
    below_out[...] = below[...].astype(BF16)
    below_out[0, 0] = (below[0, 0] + masked(pred[0] >= 0, got[1].astype(F32))).astype(BF16)


def last_kernel(pred, frames, here, got, above, out):
    for slot in range(2):
        for t in range(2):
            v = here[slot, t] + above[slot, t].astype(F32)
            if slot == 0 and t == 0:
                v = v + masked(pred[0] >= 0, got[0].astype(F32))
            out[slot, t, 0] = masked(2 * t < frames[slot], v).astype(BF16)


VMEM = pl.BlockSpec(memory_space=pltpu.VMEM)
SMEM = pl.BlockSpec(memory_space=pltpu.SMEM)


def call(kernel, outs, scratch, scalars, arrays, flops, limit=VMEM_LIMIT):
    return pl.pallas_call(
        kernel,
        out_shape=[jax.ShapeDtypeStruct(shape, dtype) for shape, dtype in outs],
        in_specs=[SMEM] * len(scalars) + [VMEM] * len(arrays),
        out_specs=[VMEM] * len(outs),
        scratch_shapes=scratch,
        compiler_params=pltpu.CompilerParams(vmem_limit_bytes=limit),
        cost_estimate=pl.CostEstimate(flops=flops, bytes_accessed=2**18, transcendentals=0),
    )(*scalars, *arrays)


def local(
    video, pred_slot, frames, gain_one, conv_one, bias_one, gain_two, conv_two, bias_two, down_weight, down_bias
):
    n_block, n_space = lax.axis_size("block"), lax.axis_size("space")
    inner = [(i, i ^ 1) for i in range(n_space)]
    outer = [(i, j) for i in range(n_space) if 0 <= (j := i + 1 if i % 2 else i - 1) < n_space]
    onward = [(b, b + 1) for b in range(n_block - 1)]
    corner = [(b * n_space + i, (b + 1) * n_space + j) for b in range(n_block - 1) for i, j in outer]
    band = video.shape
    act, tail = call(
        first_kernel, [(band, BF16), (band[1:], BF16)], [], (frames,), (video, gain_one.reshape(1, 128)), 10**9,
        60 * 2**20,
    )
    pown = lax.ppermute(tail, "block", onward)
    pin = lax.ppermute(act, "space", inner)
    cross = lax.ppermute(act, "space", outer)
    pcross = lax.ppermute(tail, ("block", "space"), corner)
    wide = ((1536, 768), BF16)
    conv_one, pown = lax.optimization_barrier((conv_one, pown))
    wide_one, wide_two = call(weight_kernel, [wide, wide], [], (), (conv_one, conv_two), WEIGHT)
    ppin = lax.ppermute(pown, "space", inner)
    norm = (wide_one, bias_one.reshape(1, 128), gain_two.reshape(1, 128))
    stride = (wide_two, bias_two.reshape(1, 128), down_weight.reshape(3, 1152, 256))

    def hidden(count, rows=4):
        return ((count, rows, 128, 128), BF16)

    def vmem(shape):
        return pltpu.VMEM(*shape)

    both = ((2, 2, 64, 256), F32)
    near, mid = call(mid_kernel, [hidden(10), hidden(6, 2)], [], (pred_slot,), (act, pin, *norm), MID)
    u2a, u2b = call(
        outer_kernel, [hidden(2), hidden(6)], [vmem(hidden(10))], (pred_slot,),
        (near, mid, cross, *norm), OUTER,
    )
    before_refs = (pown, ppin, pcross)
    bias = down_bias.reshape(1, 256)
    one = ((2, 64, 256), F32)
    ys = ((4, 2, 136, 128), F32)
    here_b, below_b, sent_b = call(
        second_kernel, [one, one, one], [vmem(ys)], (), (u2b, video, *stride, bias), SECOND
    )
    ya = ((2,) + ys[0][1:], F32)
    u2c, ya, sent = call(
        context_kernel, [hidden(2), ya, ((2, 64, 256), BF16)], [vmem(hidden(4, 6)), vmem(hidden(4)), vmem(ya)],
        (pred_slot, frames), (near, cross, *before_refs, u2a, sent_b, video, *norm, *stride), 10**9,
    )
    out, below = call(
        rest_kernel, [both, both], [vmem(hidden(4, 6)), vmem(hidden(4)), vmem(ys)], (pred_slot,),
        (*before_refs, u2c, u2a, ya, here_b, below_b, video, *norm, *stride, bias), 4 * 10**9,
    )
    got = lax.ppermute(sent, "block", onward)
    [below] = call(relay_kernel, [(both[0], BF16)], [], (pred_slot,), (got, below), 10**6)
    above = lax.ppermute(below, "space", [(i, i + 1) for i in range(n_space - 1)])
    [down] = call(last_kernel, [((2, 2, 1, 64, 256), BF16)], [], (pred_slot, frames), (out, got, above), 10**6)
    return down


def solution(mesh):
    return jax.shard_map(
        local,
        mesh=mesh,
        in_specs=(P("block", None, "space", None, None), P("block"), P("block")) + (P(),) * 8,
        out_specs=P("block", None, "space", None, None),
        check_vma=False,
    )
```

```python
import jax
import jax.numpy as jnp
from jax import lax
from jax.experimental import pallas as pl
from jax.experimental.pallas import tpu as pltpu
from jax.sharding import PartitionSpec as P

F32 = jnp.float32
BF16 = jnp.bfloat16
VMEM_LIMIT = 26 * 2**20
WEIGHT = 3 * 10**9
MID = 10**10
OUTER = 10**9
SECOND = 10**9


def activate(values, gain):
    values = values.astype(F32)
    mean = jnp.mean(values * values, axis=-1, keepdims=True)
    half = values * lax.rsqrt(mean + 1e-06) * (0.5 * gain)
    return half + half * jnp.tanh(half)


def masked(keep, value):
    return jnp.where(keep, value, jnp.zeros_like(value))


def pair_weight(weight):
    zero = jnp.zeros((128, 128), BF16)
    return jnp.concatenate(
        [
            jnp.concatenate(
                [weight[kt, j - r, kw] if 0 <= j - r <= 2 else zero for kw in range(3) for r in range(2)], axis=1
            )
            for kt in range(3)
            for j in range(4)
        ],
        axis=0,
    )


def pair_conv(source, wide, frame, count, row):
    m = count * 128
    pieces = [
        source[pl.ds(frame + kt, count), row + j].reshape(m, 128) for kt in range(3) for j in range(4)
    ]
    z = jnp.dot(jnp.concatenate(pieces, axis=1), pair_weight(wide), preferred_element_type=F32)
    left = z[:, :256].reshape(count, 128, 256)
    right = z[:, 512:].reshape(count, 128, 256)
    edge = jnp.zeros((count, 1, 256), F32)
    left = jnp.concatenate([edge, left[:, :127]], axis=1)
    right = jnp.concatenate([right[:, 1:], edge], axis=1)
    return left.reshape(m, 256) + z[:, 256:512] + right.reshape(m, 256)


def first_kernel(frames, video, gain, act, tail):
    for slot in range(2):
        for frame in range(4):
            act[slot, frame] = activate(video[slot, frame], gain[...]).astype(BF16)
    tail[...] = act[jnp.where(frames[1] > 0, 1, 0)]


def hidden_rows(source, wide, bias, gain, frame, row):
    h = pair_conv(source, wide, frame, 2, row)
    for r in range(2):
        v = activate(h[:, r * 128 : r * 128 + 128] + bias[...], gain[...])
        yield r, v.reshape(2, 128, 128)


def inside(value, top, bottom):
    space = lax.axis_index("space")
    if top:
        value = masked(space > 0, value)
    if bottom:
        value = masked(space < lax.axis_size("space") - 1, value)
    return value


def summed_rows(u2, wide, bias, frame, video, slot, first, ys, at):
    h = pair_conv(u2, wide, frame, 2, 0)
    for r in range(2):
        v = h[:, r * 128 : r * 128 + 128] + bias[...]
        y = video[slot, first : first + 2, r].reshape(256, 128).astype(F32) + v
        ys[pl.ds(at, 2), r, 8:] = y.astype(BF16).astype(F32).reshape(2, 128, 128)


def columns(ys, frame, r):
    return jnp.concatenate([ys[frame, r, pl.ds(7 + kw, 64, stride=2)].astype(BF16) for kw in range(3)], axis=1)


def mid_kernel(pred, own, pin, wide, bias_one, gain_two, near, mid):
    keep = pred[1] >= 0
    parity = lax.rem(lax.axis_index("space"), 2)
    for src, at in ((own, 2 * parity), (pin, 2 - 2 * parity)):
        for slot in range(2):
            for f in range(4):
                v = src[slot, f]
                near[6 * slot + f, pl.ds(at, 2)] = v
                if slot == 0 and f >= 2:
                    near[2 + f, pl.ds(at, 2)] = masked(keep, v)
    for frame, target in ((0, 0), (4, 2), (6, 4)):
        for r, v in hidden_rows(near, wide, bias_one, gain_two, frame, 0):
            mid[target : target + 2, r] = v.astype(BF16)


def outer_kernel(pred, near, mid, cross, wide, bias_one, gain_two, u2a, u2b, ux):
    keep = pred[1] >= 0
    parity = lax.rem(lax.axis_index("space"), 2)
    at, other = 2 * parity, 2 - 2 * parity
    ux[:, pl.ds(other, 2)] = near[:, pl.ds(at, 2)]
    for slot in range(2):
        for f in range(4):
            v = cross[slot, f]
            ux[6 * slot + f, pl.ds(at, 2)] = v
            if slot == 0 and f >= 2:
                ux[2 + f, pl.ds(at, 2)] = masked(keep, v)
    for frame, target in ((0, 0), (4, 2), (6, 4)):
        for r, v in hidden_rows(ux, wide, bias_one, gain_two, frame, 0):
            v = inside(v, r == 0, r == 1).astype(BF16)
            if target == 0:
                u2a[:, at + r] = v
                v = masked(keep, v)
            u2b[target : target + 2, at + r] = v
    u2a[:, pl.ds(other, 2)] = mid[0:2]
    u2b[0:2, pl.ds(other, 2)] = masked(keep, mid[0:2])
    u2b[2:6, pl.ds(other, 2)] = mid[2:6]


def before(refs, frame, keep, ux, at):
    parity = lax.rem(lax.axis_index("space"), 2)
    for src, row in zip(refs, (2, 4 - 4 * parity, 4 * parity)):
        ux[at, pl.ds(row, 2)] = masked(keep, src[frame])


def strided(ys, w_down):
    rows = {(f, r): columns(ys, f, r) for f in range(4) for r in range(2)}
    here, below = {}, {}
    for kt, read, goes in ((0, (0, 2), (1, 2)), (1, (1, 3), (1, 2)), (2, (0, 2), (0, 1))):
        upper, under = (jnp.concatenate([rows[f, r] for f in read], axis=0) for r in range(2))
        parts = (
            (here, jnp.dot(jnp.concatenate([upper, under], axis=1), w_down[kt, 384:], preferred_element_type=F32)),
            (below, jnp.dot(under, w_down[kt, :384], preferred_element_type=F32)),
        )
        for i, t in enumerate(goes):
            for sums, value in parts:
                part = value[i * 64 : i * 64 + 64]
                sums[t] = sums[t] + part if t in sums else part
    return here, below


def second_kernel(u2, video, wide_two, bias_two, w_down, bias_down, here_b, below_b, sent_b, ys):
    ys[:, :, :8] = jnp.zeros((4, 2, 8, 128), F32)
    for half in range(2):
        summed_rows(u2, wide_two, bias_two, 2 * half, video, 1, 2 * half, ys, 2 * half)
    here, below = strided(ys, w_down)
    for t in range(2):
        here_b[t] = here[t] + bias_down[...]
        below_b[t] = below[t]
    sent_b[0] = here[2]
    sent_b[1] = below[2]


def context_kernel(
    pred, frames, near, cross, pown, ppin, pcross, u2a, sent_b, video,
    wide, bias_one, gain_two, wide_two, bias_two, w_down,
    u2c, ya, sent,
    ux, us, ys,
):
    keep = pred[0] >= 0
    parity = lax.rem(lax.axis_index("space"), 2)
    for f in range(2):
        before((pown, ppin, pcross), 2 + f, keep, ux, f)
    ux[2:4, pl.ds(2 - 2 * parity, 4)] = near[0:2]
    ux[2:4, pl.ds(4 * parity, 2)] = cross[0, 0:2]
    us[2:4] = u2a[...]
    ys[:, :, :8] = jnp.zeros((2, 2, 8, 128), F32)
    for row in (0, 2):
        for r, v in hidden_rows(ux, wide, bias_one, gain_two, 0, row):
            us[0:2, row + r] = inside(v, row + r == 0, row + r == 3).astype(BF16)
    u2c[...] = us[0:2]
    summed_rows(us, wide_two, bias_two, 0, video, 0, 2, ys, 0)
    ya[...] = ys[...]
    here, below = 0.0, 0.0
    for kt in range(2):
        upper, under = columns(ys, kt, 0), columns(ys, kt, 1)
        both = jnp.concatenate([upper, under], axis=1)
        here = here + jnp.dot(both, w_down[kt, 384:], preferred_element_type=F32)
        below = below + jnp.dot(under, w_down[kt, :384], preferred_element_type=F32)
    second = frames[1] > 0
    sent[0] = jnp.where(second, sent_b[0], here).astype(BF16)
    sent[1] = jnp.where(second, sent_b[1], below).astype(BF16)


def rest_kernel(
    pred, pown, ppin, pcross, u2c, u2a, ya, here_b, below_b, video,
    wide, bias_one, gain_two, wide_two, bias_two, w_down, bias_down,
    out, below_out,
    ux, ua, ys,
):
    keep_a, keep_b = pred[0] >= 0, pred[1] >= 0
    for f in range(4):
        before((pown, ppin, pcross), f, keep_a, ux, f)
    ua[2:4] = u2c[...]
    ys[0:2, :, :8] = jnp.zeros((2, 2, 8, 128), F32)
    ys[2:4] = ya[...]
    for row in (0, 2):
        for r, v in hidden_rows(ux, wide, bias_one, gain_two, 0, row):
            ua[0:2, row + r] = masked(keep_a, inside(v, row + r == 0, row + r == 3)).astype(BF16)
    summed_rows(ua, wide_two, bias_two, 0, video, 0, 0, ys, 0)
    here, below = strided(ys, w_down)
    for t in range(2):
        out[0, t] = here[t] + bias_down[...]
        below_out[0, t] = below[t]
    out[1, 0] = here_b[0] + masked(keep_b, here[2])
    out[1, 1] = here_b[1]
    below_out[1, 0] = below_b[0] + masked(keep_b, below[2])
    below_out[1, 1] = below_b[1]


def relay_kernel(pred, got, below, below_out):
    below_out[...] = below[...].astype(BF16)
    below_out[0, 0] = (below[0, 0] + masked(pred[0] >= 0, got[1].astype(F32))).astype(BF16)


def last_kernel(pred, frames, here, got, above, out):
    for slot in range(2):
        for t in range(2):
            v = here[slot, t] + above[slot, t].astype(F32)
            if slot == 0 and t == 0:
                v = v + masked(pred[0] >= 0, got[0].astype(F32))
            out[slot, t, 0] = masked(2 * t < frames[slot], v).astype(BF16)


VMEM = pl.BlockSpec(memory_space=pltpu.VMEM)
SMEM = pl.BlockSpec(memory_space=pltpu.SMEM)


def call(kernel, outs, scratch, scalars, arrays, flops, limit=VMEM_LIMIT):
    return pl.pallas_call(
        kernel,
        out_shape=[jax.ShapeDtypeStruct(shape, dtype) for shape, dtype in outs],
        in_specs=[SMEM] * len(scalars) + [VMEM] * len(arrays),
        out_specs=[VMEM] * len(outs),
        scratch_shapes=scratch,
        compiler_params=pltpu.CompilerParams(vmem_limit_bytes=limit),
        cost_estimate=pl.CostEstimate(flops=flops, bytes_accessed=2**18, transcendentals=0),
    )(*scalars, *arrays)


def local(
    video, pred_slot, frames, gain_one, conv_one, bias_one, gain_two, conv_two, bias_two, down_weight, down_bias
):
    n_block, n_space = lax.axis_size("block"), lax.axis_size("space")
    inner = [(i, i ^ 1) for i in range(n_space)]
    outer = [(i, j) for i in range(n_space) if 0 <= (j := i + 1 if i % 2 else i - 1) < n_space]
    onward = [(b, b + 1) for b in range(n_block - 1)]
    band = video.shape
    act, tail = call(
        first_kernel, [(band, BF16), (band[1:], BF16)], [], (frames,), (video, gain_one.reshape(1, 128)), 10**9,
        60 * 2**20,
    )
    pown = lax.ppermute(tail, "block", onward)
    pin = lax.ppermute(act, "space", inner)
    sent_act, pin = lax.optimization_barrier((act, pin))
    cross = lax.ppermute(sent_act, "space", outer)
    norm = (conv_one, bias_one.reshape(1, 128), gain_two.reshape(1, 128))
    stride = (conv_two, bias_two.reshape(1, 128), down_weight.reshape(3, 1152, 256))

    def hidden(count, rows=4):
        return ((count, rows, 128, 128), BF16)

    def vmem(shape):
        return pltpu.VMEM(*shape)

    both = ((2, 2, 64, 256), F32)
    near, mid = call(mid_kernel, [hidden(10), hidden(6, 2)], [], (pred_slot,), (act, pin, *norm), MID)
    pown, mid = lax.optimization_barrier((pown, mid))
    ppin = lax.ppermute(pown, "space", inner)
    pcross = lax.ppermute(pown, "space", outer)
    u2a, u2b = call(
        outer_kernel, [hidden(2), hidden(6)], [vmem(hidden(10))], (pred_slot,),
        (near, mid, cross, *norm), OUTER,
    )
    before_refs = (pown, ppin, pcross)
    bias = down_bias.reshape(1, 256)
    one = ((2, 64, 256), F32)
    ys = ((4, 2, 136, 128), F32)
    here_b, below_b, sent_b = call(
        second_kernel, [one, one, one], [vmem(ys)], (), (u2b, video, *stride, bias), SECOND
    )
    ya = ((2,) + ys[0][1:], F32)
    u2c, ya, sent = call(
        context_kernel, [hidden(2), ya, ((2, 64, 256), BF16)], [vmem(hidden(4, 6)), vmem(hidden(4)), vmem(ya)],
        (pred_slot, frames), (near, cross, *before_refs, u2a, sent_b, video, *norm, *stride), 10**9,
    )
    out, below = call(
        rest_kernel, [both, both], [vmem(hidden(4, 6)), vmem(hidden(4)), vmem(ys)], (pred_slot,),
        (*before_refs, u2c, u2a, ya, here_b, below_b, video, *norm, *stride, bias), 4 * 10**9,
    )
    got = lax.ppermute(sent, "block", onward)
    [below] = call(relay_kernel, [(both[0], BF16)], [], (pred_slot,), (got, below), 10**6)
    above = lax.ppermute(below, "space", [(i, i + 1) for i in range(n_space - 1)])
    [down] = call(last_kernel, [((2, 2, 1, 64, 256), BF16)], [], (pred_slot, frames), (out, got, above), 10**6)
    return down


def solution(mesh):
    return jax.shard_map(
        local,
        mesh=mesh,
        in_specs=(P("block", None, "space", None, None), P("block"), P("block")) + (P(),) * 8,
        out_specs=P("block", None, "space", None, None),
        check_vma=False,
    )
```

```python
import jax
import jax.numpy as jnp
from jax import lax
from jax.experimental import pallas as pl
from jax.experimental.pallas import tpu as pltpu
from jax.sharding import PartitionSpec as P

F32 = jnp.float32
BF16 = jnp.bfloat16
VMEM_LIMIT = 26 * 2**20
WEIGHT = 3 * 10**9
MID = 10**10
OUTER = 10**9
SECOND = 10**9


def activate(values, gain):
    values = values.astype(F32)
    mean = jnp.mean(values * values, axis=-1, keepdims=True)
    half = values * lax.rsqrt(mean + 1e-06) * (0.5 * gain)
    return half + half * jnp.tanh(half)


def masked(keep, value):
    return jnp.where(keep, value, jnp.zeros_like(value))


def blocks(rows):
    return jnp.concatenate([jnp.concatenate(row, axis=1) for row in rows], axis=0)


def shared_weight(weight):
    return blocks(
        [[weight[kt, j - r, kw] for kw in range(3) for r in range(2)] for kt in range(3) for j in (1, 2)]
    )


def single_weight(weight, kh):
    zero = jnp.zeros((128, 128), BF16)
    return blocks(
        [
            [weight[f - t, kh, kw] if 0 <= f - t <= 2 else zero for kw in range(3) for t in range(2)]
            for f in range(4)
        ]
    )


def pair_conv(source, weight, frame, row):
    shared = [source[pl.ds(frame + kt, 2), row + j].reshape(256, 128) for kt in range(3) for j in (1, 2)]
    z = jnp.dot(jnp.concatenate(shared, axis=1), shared_weight(weight), preferred_element_type=F32)
    ends = []
    for at, kh in ((row, 0), (row + 3, 2)):
        pieces = jnp.concatenate([source[frame + f, at] for f in range(4)], axis=1)
        ends.append(jnp.dot(pieces, single_weight(weight, kh), preferred_element_type=F32))
    taps = []
    for kw in range(3):
        end = blocks([[e[:, (kw * 2 + t) * 128 : (kw * 2 + t) * 128 + 128] for e in ends] for t in range(2)])
        taps.append(z[:, kw * 256 : kw * 256 + 256] + end)
    edge = jnp.zeros((2, 1, 256), F32)
    left = jnp.concatenate([edge, taps[0].reshape(2, 128, 256)[:, :127]], axis=1)
    right = jnp.concatenate([taps[2].reshape(2, 128, 256)[:, 1:], edge], axis=1)
    return left.reshape(256, 256) + taps[1] + right.reshape(256, 256)


def first_kernel(frames, video, gain, act, tail):
    for slot in range(2):
        for frame in range(4):
            act[slot, frame] = activate(video[slot, frame], gain[...]).astype(BF16)
    tail[...] = act[jnp.where(frames[1] > 0, 1, 0)]


def hidden_rows(source, weight, bias, gain, frame, row):
    h = pair_conv(source, weight, frame, row)
    for r in range(2):
        v = activate(h[:, r * 128 : r * 128 + 128] + bias[...], gain[...])
        yield r, v.reshape(2, 128, 128)


def inside(value, top, bottom):
    space = lax.axis_index("space")
    if top:
        value = masked(space > 0, value)
    if bottom:
        value = masked(space < lax.axis_size("space") - 1, value)
    return value


def summed_rows(u2, weight, bias, frame, video, slot, first, ys, at):
    h = pair_conv(u2, weight, frame, 0)
    for r in range(2):
        v = h[:, r * 128 : r * 128 + 128] + bias[...]
        y = video[slot, first : first + 2, r].reshape(256, 128).astype(F32) + v
        ys[pl.ds(at, 2), r, 8:] = y.astype(BF16).astype(F32).reshape(2, 128, 128)


def columns(ys, frame, r):
    return jnp.concatenate([ys[frame, r, pl.ds(7 + kw, 64, stride=2)].astype(BF16) for kw in range(3)], axis=1)


def mid_kernel(pred, own, pin, w_one, bias_one, gain_two, near, mid):
    keep = pred[1] >= 0
    parity = lax.rem(lax.axis_index("space"), 2)
    for src, at in ((own, 2 * parity), (pin, 2 - 2 * parity)):
        for slot in range(2):
            for f in range(4):
                v = src[slot, f]
                near[6 * slot + f, pl.ds(at, 2)] = v
                if slot == 0 and f >= 2:
                    near[2 + f, pl.ds(at, 2)] = masked(keep, v)
    for frame, target in ((0, 0), (4, 2), (6, 4)):
        for r, v in hidden_rows(near, w_one, bias_one, gain_two, frame, 0):
            mid[target : target + 2, r] = v.astype(BF16)


def outer_kernel(pred, near, mid, cross, w_one, bias_one, gain_two, u2a, u2b, ux):
    keep = pred[1] >= 0
    parity = lax.rem(lax.axis_index("space"), 2)
    at, other = 2 * parity, 2 - 2 * parity
    ux[:, pl.ds(other, 2)] = near[:, pl.ds(at, 2)]
    for slot in range(2):
        for f in range(4):
            v = cross[slot, f]
            ux[6 * slot + f, pl.ds(at, 2)] = v
            if slot == 0 and f >= 2:
                ux[2 + f, pl.ds(at, 2)] = masked(keep, v)
    for frame, target in ((0, 0), (4, 2), (6, 4)):
        for r, v in hidden_rows(ux, w_one, bias_one, gain_two, frame, 0):
            v = inside(v, r == 0, r == 1).astype(BF16)
            if target == 0:
                u2a[:, at + r] = v
                v = masked(keep, v)
            u2b[target : target + 2, at + r] = v
    u2a[:, pl.ds(other, 2)] = mid[0:2]
    u2b[0:2, pl.ds(other, 2)] = masked(keep, mid[0:2])
    u2b[2:6, pl.ds(other, 2)] = mid[2:6]


def before(refs, frame, keep, ux, at):
    parity = lax.rem(lax.axis_index("space"), 2)
    for src, row in zip(refs, (2, 4 - 4 * parity, 4 * parity)):
        ux[at, pl.ds(row, 2)] = masked(keep, src[frame])


def strided(ys, w_down):
    rows = {(f, r): columns(ys, f, r) for f in range(4) for r in range(2)}
    here, below = {}, {}
    for kt, read, goes in ((0, (0, 2), (1, 2)), (1, (1, 3), (1, 2)), (2, (0, 2), (0, 1))):
        upper, under = (jnp.concatenate([rows[f, r] for f in read], axis=0) for r in range(2))
        parts = (
            (here, jnp.dot(jnp.concatenate([upper, under], axis=1), w_down[kt, 384:], preferred_element_type=F32)),
            (below, jnp.dot(under, w_down[kt, :384], preferred_element_type=F32)),
        )
        for i, t in enumerate(goes):
            for sums, value in parts:
                part = value[i * 64 : i * 64 + 64]
                sums[t] = sums[t] + part if t in sums else part
    return here, below


def second_kernel(u2, video, w_two, bias_two, w_down, bias_down, here_b, below_b, sent_b, ys):
    ys[:, :, :8] = jnp.zeros((4, 2, 8, 128), F32)
    for half in range(2):
        summed_rows(u2, w_two, bias_two, 2 * half, video, 1, 2 * half, ys, 2 * half)
    here, below = strided(ys, w_down)
    for t in range(2):
        here_b[t] = here[t] + bias_down[...]
        below_b[t] = below[t]
    sent_b[0] = here[2]
    sent_b[1] = below[2]


def context_kernel(
    pred, frames, near, cross, pown, ppin, pcross, u2a, sent_b, video,
    w_one, bias_one, gain_two, w_two, bias_two, w_down,
    u2c, ya, sent,
    ux, us, ys,
):
    keep = pred[0] >= 0
    parity = lax.rem(lax.axis_index("space"), 2)
    for f in range(2):
        before((pown, ppin, pcross), 2 + f, keep, ux, f)
    ux[2:4, pl.ds(2 - 2 * parity, 4)] = near[0:2]
    ux[2:4, pl.ds(4 * parity, 2)] = cross[0, 0:2]
    us[2:4] = u2a[...]
    ys[:, :, :8] = jnp.zeros((2, 2, 8, 128), F32)
    for row in (0, 2):
        for r, v in hidden_rows(ux, w_one, bias_one, gain_two, 0, row):
            us[0:2, row + r] = inside(v, row + r == 0, row + r == 3).astype(BF16)
    u2c[...] = us[0:2]
    summed_rows(us, w_two, bias_two, 0, video, 0, 2, ys, 0)
    ya[...] = ys[...]
    here, below = 0.0, 0.0
    for kt in range(2):
        upper, under = columns(ys, kt, 0), columns(ys, kt, 1)
        both = jnp.concatenate([upper, under], axis=1)
        here = here + jnp.dot(both, w_down[kt, 384:], preferred_element_type=F32)
        below = below + jnp.dot(under, w_down[kt, :384], preferred_element_type=F32)
    second = frames[1] > 0
    sent[0] = jnp.where(second, sent_b[0], here).astype(BF16)
    sent[1] = jnp.where(second, sent_b[1], below).astype(BF16)


def rest_kernel(
    pred, pown, ppin, pcross, u2c, u2a, ya, here_b, below_b, video,
    w_one, bias_one, gain_two, w_two, bias_two, w_down, bias_down,
    out, below_out,
    ux, ua, ys,
):
    keep_a, keep_b = pred[0] >= 0, pred[1] >= 0
    for f in range(4):
        before((pown, ppin, pcross), f, keep_a, ux, f)
    ua[2:4] = u2c[...]
    ys[0:2, :, :8] = jnp.zeros((2, 2, 8, 128), F32)
    ys[2:4] = ya[...]
    for row in (0, 2):
        for r, v in hidden_rows(ux, w_one, bias_one, gain_two, 0, row):
            ua[0:2, row + r] = masked(keep_a, inside(v, row + r == 0, row + r == 3)).astype(BF16)
    summed_rows(ua, w_two, bias_two, 0, video, 0, 0, ys, 0)
    here, below = strided(ys, w_down)
    for t in range(2):
        out[0, t] = here[t] + bias_down[...]
        below_out[0, t] = below[t]
    out[1, 0] = here_b[0] + masked(keep_b, here[2])
    out[1, 1] = here_b[1]
    below_out[1, 0] = below_b[0] + masked(keep_b, below[2])
    below_out[1, 1] = below_b[1]


def relay_kernel(pred, got, below, below_out):
    below_out[...] = below[...].astype(BF16)
    below_out[0, 0] = (below[0, 0] + masked(pred[0] >= 0, got[1].astype(F32))).astype(BF16)


def last_kernel(pred, frames, here, got, above, out):
    for slot in range(2):
        for t in range(2):
            v = here[slot, t] + above[slot, t].astype(F32)
            if slot == 0 and t == 0:
                v = v + masked(pred[0] >= 0, got[0].astype(F32))
            out[slot, t, 0] = masked(2 * t < frames[slot], v).astype(BF16)


VMEM = pl.BlockSpec(memory_space=pltpu.VMEM)
SMEM = pl.BlockSpec(memory_space=pltpu.SMEM)


def call(kernel, outs, scratch, scalars, arrays, flops, limit=VMEM_LIMIT):
    return pl.pallas_call(
        kernel,
        out_shape=[jax.ShapeDtypeStruct(shape, dtype) for shape, dtype in outs],
        in_specs=[SMEM] * len(scalars) + [VMEM] * len(arrays),
        out_specs=[VMEM] * len(outs),
        scratch_shapes=scratch,
        compiler_params=pltpu.CompilerParams(vmem_limit_bytes=limit),
        cost_estimate=pl.CostEstimate(flops=flops, bytes_accessed=2**18, transcendentals=0),
    )(*scalars, *arrays)


def local(
    video, pred_slot, frames, gain_one, conv_one, bias_one, gain_two, conv_two, bias_two, down_weight, down_bias
):
    n_block, n_space = lax.axis_size("block"), lax.axis_size("space")
    inner = [(i, i ^ 1) for i in range(n_space)]
    outer = [(i, j) for i in range(n_space) if 0 <= (j := i + 1 if i % 2 else i - 1) < n_space]
    onward = [(b, b + 1) for b in range(n_block - 1)]
    band = video.shape
    act, tail = call(
        first_kernel, [(band, BF16), (band[1:], BF16)], [], (frames,), (video, gain_one.reshape(1, 128)), 10**9,
        60 * 2**20,
    )
    pown = lax.ppermute(tail, "block", onward)
    pin = lax.ppermute(act, "space", inner)
    sent_act, pin = lax.optimization_barrier((act, pin))
    cross = lax.ppermute(sent_act, "space", outer)
    norm = (conv_one, bias_one.reshape(1, 128), gain_two.reshape(1, 128))
    stride = (conv_two, bias_two.reshape(1, 128), down_weight.reshape(3, 1152, 256))

    def hidden(count, rows=4):
        return ((count, rows, 128, 128), BF16)

    def vmem(shape):
        return pltpu.VMEM(*shape)

    both = ((2, 2, 64, 256), F32)
    near, mid = call(mid_kernel, [hidden(10), hidden(6, 2)], [], (pred_slot,), (act, pin, *norm), MID)
    pown, mid = lax.optimization_barrier((pown, mid))
    ppin = lax.ppermute(pown, "space", inner)
    pcross = lax.ppermute(pown, "space", outer)
    u2a, u2b = call(
        outer_kernel, [hidden(2), hidden(6)], [vmem(hidden(10))], (pred_slot,),
        (near, mid, cross, *norm), OUTER,
    )
    before_refs = (pown, ppin, pcross)
    bias = down_bias.reshape(1, 256)
    one = ((2, 64, 256), F32)
    ys = ((4, 2, 136, 128), F32)
    here_b, below_b, sent_b = call(
        second_kernel, [one, one, one], [vmem(ys)], (), (u2b, video, *stride, bias), SECOND
    )
    ya = ((2,) + ys[0][1:], F32)
    u2c, ya, sent = call(
        context_kernel, [hidden(2), ya, ((2, 64, 256), BF16)], [vmem(hidden(4, 6)), vmem(hidden(4)), vmem(ya)],
        (pred_slot, frames), (near, cross, *before_refs, u2a, sent_b, video, *norm, *stride), 10**9,
    )
    out, below = call(
        rest_kernel, [both, both], [vmem(hidden(4, 6)), vmem(hidden(4)), vmem(ys)], (pred_slot,),
        (*before_refs, u2c, u2a, ya, here_b, below_b, video, *norm, *stride, bias), 4 * 10**9,
    )
    got = lax.ppermute(sent, "block", onward)
    [below] = call(relay_kernel, [(both[0], BF16)], [], (pred_slot,), (got, below), 10**6)
    above = lax.ppermute(below, "space", [(i, i + 1) for i in range(n_space - 1)])
    [down] = call(last_kernel, [((2, 2, 1, 64, 256), BF16)], [], (pred_slot, frames), (out, got, above), 10**6)
    return down


def solution(mesh):
    return jax.shard_map(
        local,
        mesh=mesh,
        in_specs=(P("block", None, "space", None, None), P("block"), P("block")) + (P(),) * 8,
        out_specs=P("block", None, "space", None, None),
        check_vma=False,
    )
```

```python
import jax
import jax.numpy as jnp
from jax import lax
from jax.experimental import pallas as pl
from jax.experimental.pallas import tpu as pltpu
from jax.sharding import PartitionSpec as P

F32 = jnp.float32
BF16 = jnp.bfloat16
VMEM_LIMIT = 26 * 2**20
WEIGHT = 3 * 10**9
MID = 10**10
OUTER = 10**9
SECOND = 10**9


def activate(values, gain):
    values = values.astype(F32)
    mean = jnp.mean(values * values, axis=-1, keepdims=True)
    half = values * lax.rsqrt(mean + 1e-06) * (0.5 * gain)
    return half + half * jnp.tanh(half)


def masked(keep, value):
    return jnp.where(keep, value, jnp.zeros_like(value))


def blocks(rows):
    return jnp.concatenate([jnp.concatenate(row, axis=1) for row in rows], axis=0)


def shared_weight(weight):
    return blocks(
        [[weight[kt, j - r, kw] for kw in range(3) for r in range(2)] for kt in range(3) for j in (1, 2)]
    )


def single_weight(weight, kh):
    zero = jnp.zeros((128, 128), BF16)
    return blocks(
        [
            [weight[f - t, kh, kw] if 0 <= f - t <= 2 else zero for kw in range(3) for t in range(2)]
            for f in range(4)
        ]
    )


def pair_conv(source, weight, frame, row):
    shared = [source[pl.ds(frame + kt, 2), row + j].reshape(256, 128) for kt in range(3) for j in (1, 2)]
    z = jnp.dot(jnp.concatenate(shared, axis=1), shared_weight(weight), preferred_element_type=F32)
    ends = []
    for at, kh in ((row, 0), (row + 3, 2)):
        pieces = jnp.concatenate([source[frame + f, at] for f in range(4)], axis=1)
        ends.append(jnp.dot(pieces, single_weight(weight, kh), preferred_element_type=F32))
    taps = []
    for kw in range(3):
        end = blocks([[e[:, (kw * 2 + t) * 128 : (kw * 2 + t) * 128 + 128] for e in ends] for t in range(2)])
        taps.append(z[:, kw * 256 : kw * 256 + 256] + end)
    edge = jnp.zeros((2, 1, 256), F32)
    left = jnp.concatenate([edge, taps[0].reshape(2, 128, 256)[:, :127]], axis=1)
    right = jnp.concatenate([taps[2].reshape(2, 128, 256)[:, 1:], edge], axis=1)
    return left.reshape(256, 256) + taps[1] + right.reshape(256, 256)


def first_kernel(frames, video, gain, act, tail):
    for slot in range(2):
        for frame in range(4):
            act[slot, frame] = activate(video[slot, frame], gain[...]).astype(BF16)
    tail[...] = act[jnp.where(frames[1] > 0, 1, 0)]


def hidden_rows(source, weight, bias, gain, frame, row):
    h = pair_conv(source, weight, frame, row)
    for r in range(2):
        v = activate(h[:, r * 128 : r * 128 + 128] + bias[...], gain[...])
        yield r, v.reshape(2, 128, 128)


def inside(value, top, bottom):
    space = lax.axis_index("space")
    if top:
        value = masked(space > 0, value)
    if bottom:
        value = masked(space < lax.axis_size("space") - 1, value)
    return value


def summed_rows(u2, weight, bias, frame, video, slot, first, ys, at):
    h = pair_conv(u2, weight, frame, 0)
    for r in range(2):
        v = h[:, r * 128 : r * 128 + 128] + bias[...]
        y = video[slot, first : first + 2, r].reshape(256, 128).astype(F32) + v
        ys[pl.ds(at, 2), r, 8:] = y.astype(BF16).astype(F32).reshape(2, 128, 128)


def columns(ys, frame, r):
    return jnp.concatenate([ys[frame, r, pl.ds(7 + kw, 64, stride=2)].astype(BF16) for kw in range(3)], axis=1)


def mid_kernel(pred, own, pin, w_one, bias_one, gain_two, near, mid):
    keep = pred[1] >= 0
    parity = lax.rem(lax.axis_index("space"), 2)
    for src, at in ((own, 2 * parity), (pin, 2 - 2 * parity)):
        for slot in range(2):
            for f in range(4):
                v = src[slot, f]
                near[6 * slot + f, pl.ds(at, 2)] = v
                if slot == 0 and f >= 2:
                    near[2 + f, pl.ds(at, 2)] = masked(keep, v)
    for frame, target in ((0, 0), (4, 2), (6, 4)):
        for r, v in hidden_rows(near, w_one, bias_one, gain_two, frame, 0):
            mid[target : target + 2, r] = v.astype(BF16)


def outer_kernel(pred, near, mid, cross, w_one, bias_one, gain_two, u2a, u2b, ux):
    keep = pred[1] >= 0
    parity = lax.rem(lax.axis_index("space"), 2)
    at, other = 2 * parity, 2 - 2 * parity
    ux[:, pl.ds(other, 2)] = near[:, pl.ds(at, 2)]
    for slot in range(2):
        for f in range(4):
            v = cross[slot, f]
            ux[6 * slot + f, pl.ds(at, 2)] = v
            if slot == 0 and f >= 2:
                ux[2 + f, pl.ds(at, 2)] = masked(keep, v)
    for frame, target in ((0, 0), (4, 2), (6, 4)):
        for r, v in hidden_rows(ux, w_one, bias_one, gain_two, frame, 0):
            v = inside(v, r == 0, r == 1).astype(BF16)
            if target == 0:
                u2a[:, at + r] = v
                v = masked(keep, v)
            u2b[target : target + 2, at + r] = v
    u2a[:, pl.ds(other, 2)] = mid[0:2]
    u2b[0:2, pl.ds(other, 2)] = masked(keep, mid[0:2])
    u2b[2:6, pl.ds(other, 2)] = mid[2:6]


def before(refs, frame, keep, ux, at):
    parity = lax.rem(lax.axis_index("space"), 2)
    for src, row in zip(refs, (2, 4 - 4 * parity, 4 * parity)):
        ux[at, pl.ds(row, 2)] = masked(keep, src[frame])


def strided(ys, w_down):
    rows = {(f, r): columns(ys, f, r) for f in range(4) for r in range(2)}
    here, below = {}, {}
    for kt, read, goes in ((0, (0, 2), (1, 2)), (1, (1, 3), (1, 2)), (2, (0, 2), (0, 1))):
        upper, under = (jnp.concatenate([rows[f, r] for f in read], axis=0) for r in range(2))
        parts = (
            (here, jnp.dot(jnp.concatenate([upper, under], axis=1), w_down[kt, 384:], preferred_element_type=F32)),
            (below, jnp.dot(under, w_down[kt, :384], preferred_element_type=F32)),
        )
        for i, t in enumerate(goes):
            for sums, value in parts:
                part = value[i * 64 : i * 64 + 64]
                sums[t] = sums[t] + part if t in sums else part
    return here, below


def second_kernel(u2, video, w_two, bias_two, w_down, bias_down, here_b, below_b, sent_b, ys):
    ys[:, :, :8] = jnp.zeros((4, 2, 8, 128), F32)
    for half in range(2):
        summed_rows(u2, w_two, bias_two, 2 * half, video, 1, 2 * half, ys, 2 * half)
    here, below = strided(ys, w_down)
    for t in range(2):
        here_b[t] = here[t] + bias_down[...]
        below_b[t] = below[t]
    sent_b[0] = here[2]
    sent_b[1] = below[2]


def context_kernel(
    pred, frames, near, cross, pown, ppin, pcross, u2a, sent_b, video,
    w_one, bias_one, gain_two, w_two, bias_two, w_down,
    u2c, ya, sent,
    ux, us, ys,
):
    keep = pred[0] >= 0
    parity = lax.rem(lax.axis_index("space"), 2)
    for f in range(2):
        before((pown, ppin, pcross), 2 + f, keep, ux, f)
    ux[2:4, pl.ds(2 - 2 * parity, 4)] = near[0:2]
    ux[2:4, pl.ds(4 * parity, 2)] = cross[0, 0:2]
    us[2:4] = u2a[...]
    ys[:, :, :8] = jnp.zeros((2, 2, 8, 128), F32)
    for row in (0, 2):
        for r, v in hidden_rows(ux, w_one, bias_one, gain_two, 0, row):
            us[0:2, row + r] = inside(v, row + r == 0, row + r == 3).astype(BF16)
    u2c[...] = us[0:2]
    summed_rows(us, w_two, bias_two, 0, video, 0, 2, ys, 0)
    ya[...] = ys[...]
    here, below = 0.0, 0.0
    for kt in range(2):
        upper, under = columns(ys, kt, 0), columns(ys, kt, 1)
        both = jnp.concatenate([upper, under], axis=1)
        here = here + jnp.dot(both, w_down[kt, 384:], preferred_element_type=F32)
        below = below + jnp.dot(under, w_down[kt, :384], preferred_element_type=F32)
    second = frames[1] > 0
    sent[0] = jnp.where(second, sent_b[0], here).astype(BF16)
    sent[1] = jnp.where(second, sent_b[1], below).astype(BF16)


def rest_kernel(
    pred, pown, ppin, pcross, u2c, u2a, ya, here_b, below_b, video,
    w_one, bias_one, gain_two, w_two, bias_two, w_down, bias_down,
    out, below_out,
    ux, ua, ys,
):
    keep_a, keep_b = pred[0] >= 0, pred[1] >= 0
    for f in range(4):
        before((pown, ppin, pcross), f, keep_a, ux, f)
    ua[2:4] = u2c[...]
    ys[0:2, :, :8] = jnp.zeros((2, 2, 8, 128), F32)
    ys[2:4] = ya[...]
    for row in (0, 2):
        for r, v in hidden_rows(ux, w_one, bias_one, gain_two, 0, row):
            ua[0:2, row + r] = masked(keep_a, inside(v, row + r == 0, row + r == 3)).astype(BF16)
    summed_rows(ua, w_two, bias_two, 0, video, 0, 0, ys, 0)
    here, below = strided(ys, w_down)
    for t in range(2):
        out[0, t] = here[t] + bias_down[...]
        below_out[0, t] = below[t].astype(BF16)
    out[1, 0] = here_b[0] + masked(keep_b, here[2])
    out[1, 1] = here_b[1]
    below_out[1, 0] = (below_b[0] + masked(keep_b, below[2])).astype(BF16)
    below_out[1, 1] = below_b[1].astype(BF16)


def last_kernel(pred, frames, here, got, above, passed, out):
    for slot in range(2):
        for t in range(2):
            v = here[slot, t] + above[slot, t].astype(F32)
            if slot == 0 and t == 0:
                v = v + masked(pred[0] >= 0, got[0].astype(F32) + passed[1].astype(F32))
            out[slot, t, 0] = masked(2 * t < frames[slot], v).astype(BF16)


VMEM = pl.BlockSpec(memory_space=pltpu.VMEM)
SMEM = pl.BlockSpec(memory_space=pltpu.SMEM)


def call(kernel, outs, scratch, scalars, arrays, flops, limit=VMEM_LIMIT):
    return pl.pallas_call(
        kernel,
        out_shape=[jax.ShapeDtypeStruct(shape, dtype) for shape, dtype in outs],
        in_specs=[SMEM] * len(scalars) + [VMEM] * len(arrays),
        out_specs=[VMEM] * len(outs),
        scratch_shapes=scratch,
        compiler_params=pltpu.CompilerParams(vmem_limit_bytes=limit),
        cost_estimate=pl.CostEstimate(flops=flops, bytes_accessed=2**18, transcendentals=0),
    )(*scalars, *arrays)


def local(
    video, pred_slot, frames, gain_one, conv_one, bias_one, gain_two, conv_two, bias_two, down_weight, down_bias
):
    n_block, n_space = lax.axis_size("block"), lax.axis_size("space")
    inner = [(i, i ^ 1) for i in range(n_space)]
    outer = [(i, j) for i in range(n_space) if 0 <= (j := i + 1 if i % 2 else i - 1) < n_space]
    onward = [(b, b + 1) for b in range(n_block - 1)]
    band = video.shape
    act, tail = call(
        first_kernel, [(band, BF16), (band[1:], BF16)], [], (frames,), (video, gain_one.reshape(1, 128)), 10**9,
        60 * 2**20,
    )
    pown = lax.ppermute(tail, "block", onward)
    pin = lax.ppermute(act, "space", inner)
    sent_act, pin = lax.optimization_barrier((act, pin))
    cross = lax.ppermute(sent_act, "space", outer)
    norm = (conv_one, bias_one.reshape(1, 128), gain_two.reshape(1, 128))
    stride = (conv_two, bias_two.reshape(1, 128), down_weight.reshape(3, 1152, 256))

    def hidden(count, rows=4):
        return ((count, rows, 128, 128), BF16)

    def vmem(shape):
        return pltpu.VMEM(*shape)

    both = ((2, 2, 64, 256), F32)
    near, mid = call(mid_kernel, [hidden(10), hidden(6, 2)], [], (pred_slot,), (act, pin, *norm), MID)
    pown, mid = lax.optimization_barrier((pown, mid))
    ppin = lax.ppermute(pown, "space", inner)
    pcross = lax.ppermute(pown, "space", outer)
    u2a, u2b = call(
        outer_kernel, [hidden(2), hidden(6)], [vmem(hidden(10))], (pred_slot,),
        (near, mid, cross, *norm), OUTER,
    )
    before_refs = (pown, ppin, pcross)
    bias = down_bias.reshape(1, 256)
    one = ((2, 64, 256), F32)
    ys = ((4, 2, 136, 128), F32)
    here_b, below_b, sent_b = call(
        second_kernel, [one, one, one], [vmem(ys)], (), (u2b, video, *stride, bias), SECOND
    )
    ya = ((2,) + ys[0][1:], F32)
    u2c, ya, sent = call(
        context_kernel, [hidden(2), ya, ((2, 64, 256), BF16)], [vmem(hidden(4, 6)), vmem(hidden(4)), vmem(ya)],
        (pred_slot, frames), (near, cross, *before_refs, u2a, sent_b, video, *norm, *stride), 10**9,
    )
    out, below = call(
        rest_kernel, [both, (both[0], BF16)], [vmem(hidden(4, 6)), vmem(hidden(4)), vmem(ys)], (pred_slot,),
        (*before_refs, u2c, u2a, ya, here_b, below_b, video, *norm, *stride, bias), 4 * 10**9,
    )
    downward = [(i, i + 1) for i in range(n_space - 1)]
    above = lax.ppermute(below, "space", downward)
    got = lax.ppermute(sent, "block", onward)
    passed = lax.ppermute(got, "space", downward)
    [down] = call(
        last_kernel, [((2, 2, 1, 64, 256), BF16)], [], (pred_slot, frames), (out, got, above, passed), 10**6
    )
    return down


def solution(mesh):
    return jax.shard_map(
        local,
        mesh=mesh,
        in_specs=(P("block", None, "space", None, None), P("block"), P("block")) + (P(),) * 8,
        out_specs=P("block", None, "space", None, None),
        check_vma=False,
    )
```

```python
import jax
import jax.numpy as jnp
from jax import lax
from jax.experimental import pallas as pl
from jax.experimental.pallas import tpu as pltpu
from jax.sharding import PartitionSpec as P

F32 = jnp.float32
BF16 = jnp.bfloat16
VMEM_LIMIT = 26 * 2**20
WEIGHT = 3 * 10**9
MID = 10**10
OUTER = 10**9
SECOND = 10**9


def activate(values, gain):
    values = values.astype(F32)
    mean = jnp.mean(values * values, axis=-1, keepdims=True)
    half = values * lax.rsqrt(mean + 1e-06) * (0.5 * gain)
    return half + half * jnp.tanh(half)


def masked(keep, value):
    return jnp.where(keep, value, jnp.zeros_like(value))


def blocks(rows):
    return jnp.concatenate([jnp.concatenate(row, axis=1) for row in rows], axis=0)


def shared_weight(weight):
    return blocks(
        [[weight[kt, j - r, kw] for kw in range(3) for r in range(2)] for kt in range(3) for j in (1, 2)]
    )


def single_weight(weight, kh):
    zero = jnp.zeros((128, 128), BF16)
    return blocks(
        [
            [weight[f - t, kh, kw] if 0 <= f - t <= 2 else zero for kw in range(3) for t in range(2)]
            for f in range(4)
        ]
    )


def pair_conv(source, weight, frame, row):
    shared = [source[pl.ds(frame + kt, 2), row + j].reshape(256, 128) for kt in range(3) for j in (1, 2)]
    z = jnp.dot(jnp.concatenate(shared, axis=1), shared_weight(weight), preferred_element_type=F32)
    ends = []
    for at, kh in ((row, 0), (row + 3, 2)):
        pieces = jnp.concatenate([source[frame + f, at] for f in range(4)], axis=1)
        ends.append(jnp.dot(pieces, single_weight(weight, kh), preferred_element_type=F32))
    taps = []
    for kw in range(3):
        end = blocks([[e[:, (kw * 2 + t) * 128 : (kw * 2 + t) * 128 + 128] for e in ends] for t in range(2)])
        taps.append(z[:, kw * 256 : kw * 256 + 256] + end)
    edge = jnp.zeros((2, 1, 256), F32)
    left = jnp.concatenate([edge, taps[0].reshape(2, 128, 256)[:, :127]], axis=1)
    right = jnp.concatenate([taps[2].reshape(2, 128, 256)[:, 1:], edge], axis=1)
    return left.reshape(256, 256) + taps[1] + right.reshape(256, 256)


def first_kernel(frames, video, gain, act, tail):
    for slot in range(2):
        for frame in range(4):
            act[slot, frame] = activate(video[slot, frame], gain[...]).astype(BF16)
    tail[...] = act[jnp.where(frames[1] > 0, 1, 0)]


def hidden_rows(source, weight, bias, gain, frame, row):
    h = pair_conv(source, weight, frame, row)
    for r in range(2):
        v = activate(h[:, r * 128 : r * 128 + 128] + bias[...], gain[...])
        yield r, v.reshape(2, 128, 128)


def inside(value, top, bottom):
    space = lax.axis_index("space")
    if top:
        value = masked(space > 0, value)
    if bottom:
        value = masked(space < lax.axis_size("space") - 1, value)
    return value


def summed_rows(u2, weight, bias, frame, video, slot, first, ys, at):
    h = pair_conv(u2, weight, frame, 0)
    for r in range(2):
        v = h[:, r * 128 : r * 128 + 128] + bias[...]
        y = video[slot, first : first + 2, r].reshape(256, 128).astype(F32) + v
        ys[pl.ds(at, 2), r, 8:] = y.astype(BF16).astype(F32).reshape(2, 128, 128)


def columns(ys, frame, r):
    return jnp.concatenate([ys[frame, r, pl.ds(7 + kw, 64, stride=2)].astype(BF16) for kw in range(3)], axis=1)


def mid_kernel(pred, own, pin, w_one, bias_one, gain_two, near, mid):
    keep = pred[1] >= 0
    parity = lax.rem(lax.axis_index("space"), 2)
    for src, at in ((own, 2 * parity), (pin, 2 - 2 * parity)):
        for slot in range(2):
            for f in range(4):
                v = src[slot, f]
                near[6 * slot + f, pl.ds(at, 2)] = v
                if slot == 0 and f >= 2:
                    near[2 + f, pl.ds(at, 2)] = masked(keep, v)
    for frame, target in ((0, 0), (4, 2), (6, 4)):
        for r, v in hidden_rows(near, w_one, bias_one, gain_two, frame, 0):
            mid[target : target + 2, r] = v.astype(BF16)


def outer_kernel(pred, near, mid, cross, w_one, bias_one, gain_two, u2a, u2b, ux):
    keep = pred[1] >= 0
    parity = lax.rem(lax.axis_index("space"), 2)
    at, other = 2 * parity, 2 - 2 * parity
    ux[:, pl.ds(other, 2)] = near[:, pl.ds(at, 2)]
    for slot in range(2):
        for f in range(4):
            v = cross[slot, f]
            ux[6 * slot + f, pl.ds(at, 2)] = v
            if slot == 0 and f >= 2:
                ux[2 + f, pl.ds(at, 2)] = masked(keep, v)
    for frame, target in ((0, 0), (4, 2), (6, 4)):
        for r, v in hidden_rows(ux, w_one, bias_one, gain_two, frame, 0):
            v = inside(v, r == 0, r == 1).astype(BF16)
            if target == 0:
                u2a[:, at + r] = v
                v = masked(keep, v)
            u2b[target : target + 2, at + r] = v
    u2a[:, pl.ds(other, 2)] = mid[0:2]
    u2b[0:2, pl.ds(other, 2)] = masked(keep, mid[0:2])
    u2b[2:6, pl.ds(other, 2)] = mid[2:6]


def before(refs, frame, keep, ux, at):
    parity = lax.rem(lax.axis_index("space"), 2)
    for src, row in zip(refs, (2, 4 - 4 * parity, 4 * parity)):
        ux[at, pl.ds(row, 2)] = masked(keep, src[frame])


READS = ((0, (0,), (1,)), (1, (1,), (1,)), (2, (0, 2), (0, 1)))


def strided(slots, w_down, part):
    sums = {}
    for kt, read, goes in READS:
        under = jnp.concatenate([columns(ys, f, 1) for ys in slots for f in read], axis=0)
        if part == 0:
            upper = jnp.concatenate([columns(ys, f, 0) for ys in slots for f in read], axis=0)
            under, weight = jnp.concatenate([upper, under], axis=1), w_down[kt, 384:]
        else:
            weight = w_down[kt, :384]
        value = jnp.dot(under, weight, preferred_element_type=F32)
        for slot in range(2):
            for i, t in enumerate(goes):
                at = (slot * len(read) + i) * 64
                piece = value[at : at + 64]
                sums[slot, t] = sums[slot, t] + piece if (slot, t) in sums else piece
    return sums


def successor(ys, frame, w_down):
    here, below = 0.0, 0.0
    for kt in range(2):
        upper, under = columns(ys, frame + kt, 0), columns(ys, frame + kt, 1)
        both = jnp.concatenate([upper, under], axis=1)
        here = here + jnp.dot(both, w_down[kt, 384:], preferred_element_type=F32)
        below = below + jnp.dot(under, w_down[kt, :384], preferred_element_type=F32)
    return here, below


def second_kernel(u2, video, w_two, bias_two, w_down, ys, sent_b):
    ys[:, :, :8] = jnp.zeros((4, 2, 8, 128), F32)
    for half in (1, 0):
        summed_rows(u2, w_two, bias_two, 2 * half, video, 1, 2 * half, ys, 2 * half)
    sent_b[0], sent_b[1] = successor(ys, 2, w_down)


def context_kernel(
    pred, frames, near, cross, pown, ppin, pcross, u2a, sent_b, video,
    w_one, bias_one, gain_two, w_two, bias_two, w_down,
    u2c, ys, sent, sent_a,
    ux, us,
):
    keep = pred[0] >= 0
    parity = lax.rem(lax.axis_index("space"), 2)
    for f in range(2):
        before((pown, ppin, pcross), 2 + f, keep, ux, f)
    ux[2:4, pl.ds(2 - 2 * parity, 4)] = near[0:2]
    ux[2:4, pl.ds(4 * parity, 2)] = cross[0, 0:2]
    us[2:4] = u2a[...]
    ys[:, :, :8] = jnp.zeros((2, 2, 8, 128), F32)
    for row in (0, 2):
        for r, v in hidden_rows(ux, w_one, bias_one, gain_two, 0, row):
            us[0:2, row + r] = inside(v, row + r == 0, row + r == 3).astype(BF16)
    u2c[...] = us[0:2]
    summed_rows(us, w_two, bias_two, 0, video, 0, 2, ys, 0)
    here, below = successor(ys, 0, w_down)
    sent_a[0] = here
    sent_a[1] = below
    second = frames[1] > 0
    sent[0] = jnp.where(second, sent_b[0], here).astype(BF16)
    sent[1] = jnp.where(second, sent_b[1], below).astype(BF16)


def rest_kernel(
    pred, pown, ppin, pcross, u2c, ya, video, w_one, bias_one, gain_two, w_two, bias_two, ys, ux, ua
):
    keep = pred[0] >= 0
    for f in range(4):
        before((pown, ppin, pcross), f, keep, ux, f)
    ua[2:4] = u2c[...]
    ys[0:2, :, :8] = jnp.zeros((2, 2, 8, 128), F32)
    ys[2:4] = ya[...]
    for row in (0, 2):
        for r, v in hidden_rows(ux, w_one, bias_one, gain_two, 0, row):
            ua[0:2, row + r] = masked(keep, inside(v, row + r == 0, row + r == 3)).astype(BF16)
    summed_rows(ua, w_two, bias_two, 0, video, 0, 0, ys, 0)


def joined(pred, sums, sent_a, got, part):
    sums[0, 0] += masked(pred[0] >= 0, got[part].astype(F32))
    sums[1, 0] += masked(pred[1] >= 0, sent_a[part])
    return sums


def relay_kernel(pred, ysa, ysb, sent_a, got, w_down, below):
    sums = joined(pred, strided((ysa, ysb), w_down, 1), sent_a, got, 1)
    for slot in range(2):
        for t in range(2):
            below[slot, t] = sums[slot, t].astype(BF16)


def here_kernel(pred, ysa, ysb, sent_a, got, w_down, bias_down, out):
    sums = joined(pred, strided((ysa, ysb), w_down, 0), sent_a, got, 0)
    for slot in range(2):
        for t in range(2):
            out[slot, t] = sums[slot, t] + bias_down[...]


def last_kernel(frames, here, above, out):
    for slot in range(2):
        for t in range(2):
            v = here[slot, t] + above[slot, t].astype(F32)
            out[slot, t, 0] = masked(2 * t < frames[slot], v).astype(BF16)


VMEM = pl.BlockSpec(memory_space=pltpu.VMEM)
SMEM = pl.BlockSpec(memory_space=pltpu.SMEM)


def call(kernel, outs, scratch, scalars, arrays, flops, limit=VMEM_LIMIT):
    return pl.pallas_call(
        kernel,
        out_shape=[jax.ShapeDtypeStruct(shape, dtype) for shape, dtype in outs],
        in_specs=[SMEM] * len(scalars) + [VMEM] * len(arrays),
        out_specs=[VMEM] * len(outs),
        scratch_shapes=scratch,
        compiler_params=pltpu.CompilerParams(vmem_limit_bytes=limit),
        cost_estimate=pl.CostEstimate(flops=flops, bytes_accessed=2**18, transcendentals=0),
    )(*scalars, *arrays)


def local(
    video, pred_slot, frames, gain_one, conv_one, bias_one, gain_two, conv_two, bias_two, down_weight, down_bias
):
    n_block, n_space = lax.axis_size("block"), lax.axis_size("space")
    inner = [(i, i ^ 1) for i in range(n_space)]
    outer = [(i, j) for i in range(n_space) if 0 <= (j := i + 1 if i % 2 else i - 1) < n_space]
    onward = [(b, b + 1) for b in range(n_block - 1)]
    band = video.shape
    act, tail = call(
        first_kernel, [(band, BF16), (band[1:], BF16)], [], (frames,), (video, gain_one.reshape(1, 128)), 10**9,
        60 * 2**20,
    )
    pown = lax.ppermute(tail, "block", onward)
    pin = lax.ppermute(act, "space", inner)
    sent_act, pin = lax.optimization_barrier((act, pin))
    cross = lax.ppermute(sent_act, "space", outer)
    norm = (conv_one, bias_one.reshape(1, 128), gain_two.reshape(1, 128))
    stride = (conv_two, bias_two.reshape(1, 128), down_weight.reshape(3, 1152, 256))

    def hidden(count, rows=4):
        return ((count, rows, 128, 128), BF16)

    def vmem(shape):
        return pltpu.VMEM(*shape)

    both = ((2, 2, 64, 256), F32)
    near, mid = call(mid_kernel, [hidden(10), hidden(6, 2)], [], (pred_slot,), (act, pin, *norm), MID)
    pown, mid = lax.optimization_barrier((pown, mid))
    ppin = lax.ppermute(pown, "space", inner)
    pcross = lax.ppermute(pown, "space", outer)
    u2a, u2b = call(
        outer_kernel, [hidden(2), hidden(6)], [vmem(hidden(10))], (pred_slot,),
        (near, mid, cross, *norm), OUTER,
    )
    before_refs = (pown, ppin, pcross)
    down_weight = down_weight.reshape(3, 1152, 256)
    pair = ((2, 64, 256), F32)
    ys = ((4, 2, 136, 128), F32)
    ya = ((2,) + ys[0][1:], F32)
    ysb, sent_b = call(second_kernel, [ys, pair], [], (), (u2b, video, *stride), SECOND)
    u2c, ya, sent, sent_a = call(
        context_kernel, [hidden(2), ya, (pair[0], BF16), pair], [vmem(hidden(4, 6)), vmem(hidden(4))],
        (pred_slot, frames), (near, cross, *before_refs, u2a, sent_b, video, *norm, *stride), 10**9,
    )
    [ysa] = call(
        rest_kernel, [ys], [vmem(hidden(4, 6)), vmem(hidden(4))], (pred_slot,),
        (*before_refs, u2c, ya, video, *norm, *stride[:2]), 4 * 10**9,
    )
    got = lax.ppermute(sent, "block", onward)
    ends = (ysa, ysb, sent_a, got, down_weight)
    [below] = call(relay_kernel, [(both[0], BF16)], [], (pred_slot,), ends, 10**6)
    above = lax.ppermute(below, "space", [(i, i + 1) for i in range(n_space - 1)])
    [out] = call(here_kernel, [both], [], (pred_slot,), (*ends, down_bias.reshape(1, 256)), 10**9)
    [down] = call(last_kernel, [((2, 2, 1, 64, 256), BF16)], [], (frames,), (out, above), 10**6)
    return down


def solution(mesh):
    return jax.shard_map(
        local,
        mesh=mesh,
        in_specs=(P("block", None, "space", None, None), P("block"), P("block")) + (P(),) * 8,
        out_specs=P("block", None, "space", None, None),
        check_vma=False,
    )
```
